32 devices in a mesh: rows: 8 (over y, x, core), cols: 4 (over z).
Axes of the slice: x: 2, y: 2, z: 4, core: 2. Of those that a mesh axis runs over, the one named last changes fastest.
Arguments:
- feat_left: bfloat16 [128, 1024, 256], P('rows', 'cols'), may hold values from -6 to 6
- feat_right: bfloat16 [128, 1024, 256], P('rows', 'cols'), may hold values from -6 to 6
- hidden: bfloat16 [128, 1024, 128], P('rows', 'cols'), may hold values from -1 to 1
- disparity: int32 [128, 1024], P('rows', 'cols'), may hold values from 0 to 127
- motion_weight: bfloat16 [9, 128], replicated, may hold values from -2 to 2
- gate_weight: bfloat16 [3, 3, 256, 256], replicated, may hold values from -0.125 to 0.125
- cand_weight: bfloat16 [3, 3, 256, 128], replicated, may hold values from -0.125 to 0.125
- grad_hidden: bfloat16 [128, 1024, 128], P('rows', 'cols'), may hold values from -6 to 6
Outputs:
- new_hidden: bfloat16 [128, 1024, 128], P('rows', 'cols')
- grad_left: bfloat16 [128, 1024, 256], P('rows', 'cols')
- grad_right: bfloat16 [128, 1024, 256], P('rows', 'cols')
The draws below stay inside these ranges and needn't reach their ends.
Inputs may be any that keep to these rules, and one draw needn't show every extreme that they name: Whole disparity levels.
All inputs are finite; a program needn't handle non-finite values.
Results may differ from the reference program's by a relative error of at most 0.0075.
Values may be sent and summed in bfloat16 or wider, within the bound.
A program may use at most 192 MiB of HBM per device.

```python
import math
import jax
import jax.numpy as jnp
from jax import lax

C = 256
HID = 128
MOT = 128
DISP = 128
RAD = 4
TAPS = 9
HEIGHT = 128
WIDTH = 1024


def set_ends(values, stream_key, low, largest):
    longest = values.shape.index(max(values.shape))
    spots = []
    for shift in (0, 1):
        where = [jax.random.randint(jax.random.fold_in(stream_key, axis), (), 0, length) for axis, length in enumerate(values.shape)]
        where[longest] = (where[longest] + shift) % values.shape[longest]
        spots.append(tuple(where))
    return values.at[spots[0]].set(low).at[spots[1]].set(largest)


def level_of(rng, shape, cuts, least, high):
    def one(dim, blocks):
        draws = jax.random.uniform(jax.random.fold_in(jax.random.fold_in(rng, 6), dim), (blocks,), jnp.float32, least / len(cuts), high / len(cuts))
        return jnp.repeat(jnp.exp(draws), shape[dim] // blocks).reshape((-1,) + (1,) * (len(shape) - dim - 1))

    level = one(*cuts[0])
    for cut in cuts[1:]:
        level = level * one(*cut)
    return level


def centred(rng, dims, scale, limit, shards=(), kind=jnp.bfloat16):
    level = level_of(rng, dims, shards, -0.22, 0.18) if shards else 1.0
    entries = jax.random.normal(rng, dims, jnp.float32) * scale * level
    return jnp.minimum(jnp.maximum(entries, -limit), limit).astype(kind)


def setup_inputs(seed: int = 0) -> dict:
    streams_of = jax.random.split(jax.random.key(seed), 9)
    feat_left = centred(streams_of[0], (HEIGHT, WIDTH, C), 1.0, 6.0, ((0, 8), (1, 4)))
    feat_right = centred(streams_of[1], (HEIGHT, WIDTH, C), 1.0, 6.0, ((0, 8), (1, 4)))
    hidden = jnp.clip(jax.random.uniform(streams_of[2], (HEIGHT, WIDTH, HID), jnp.float32, -1.0, 1.0) * level_of(streams_of[2], (HEIGHT, WIDTH, HID), ((0, 8), (1, 4)), -0.4, 0.0), -1.0, 1.0).astype(jnp.bfloat16)
    disparity = set_ends(jax.random.randint(streams_of[3], (HEIGHT, WIDTH), 0, DISP), jax.random.fold_in(streams_of[3], 1), 0, DISP - 1).astype(jnp.int32)
    motion_weight = centred(streams_of[4], (TAPS, MOT), TAPS ** -0.5, 2.0)
    gate_weight = centred(streams_of[5], (3, 3, HID + MOT, 2 * HID), (9 * (HID + MOT)) ** -0.5, 0.125)
    cand_weight = centred(streams_of[6], (3, 3, HID + MOT, HID), (9 * (HID + MOT)) ** -0.5, 0.125)
    grad_hidden = centred(streams_of[7], (HEIGHT, WIDTH, HID), 1.0, 6.0, ((0, 8), (1, 4)))
    return dict(feat_left=feat_left, feat_right=feat_right, hidden=hidden, disparity=disparity, motion_weight=motion_weight, gate_weight=gate_weight, cand_weight=cand_weight, grad_hidden=grad_hidden)


def band_windows(feat_right, band_size):
    row_count, col_count, chan_count = feat_right.shape
    extended = jnp.concatenate([jnp.zeros((row_count, band_size, chan_count), feat_right.dtype), feat_right], axis=1)
    blocks = extended.reshape(row_count, col_count // band_size + 1, band_size, chan_count)
    return jnp.concatenate([blocks[:, :-1], blocks[:, 1:]], axis=2)

def tap_index(disparity, band_size, radius):
    col_count = disparity.shape[1]
    inner = jnp.arange(col_count, dtype=jnp.int32) % band_size
    offsets = jnp.arange(2 * radius + 1, dtype=jnp.int32) - radius
    levels = disparity[:, :, None].astype(jnp.int32) + offsets[None, None, :]
    usable = (levels >= 0) & (levels < band_size)
    columns = jnp.clip(inner[None, :, None] + band_size - levels, 0, 2 * band_size - 1)
    return (columns.astype(jnp.int32), usable)

def conv_ref(padded, weight, row_count, col_count):
    result = jnp.zeros((row_count, col_count, weight.shape[3]), jnp.float32)
    for row_off in range(3):
        for col_off in range(3):
            result = result + jnp.einsum('hwi,io->hwo', padded[row_off:row_off + row_count, col_off:col_off + col_count].astype(jnp.float32), weight[row_off, col_off].astype(jnp.float32))
    return result

def flipped(weight):
    return jnp.transpose(weight[::-1, ::-1], (0, 1, 3, 2))

def pad_grid(field):
    return jnp.pad(field, ((1, 1), (1, 1), (0, 0)))

def reference(feat_left, feat_right, hidden, disparity, motion_weight, gate_weight, cand_weight, grad_hidden):
    row_count, col_count, chan_count = feat_left.shape
    scale = 1.0 / math.sqrt(chan_count)
    block_count = col_count // DISP
    windows = band_windows(feat_right, DISP).astype(jnp.float32)
    left_blocks = feat_left.reshape(row_count, block_count, DISP, chan_count).astype(jnp.float32)
    scores = jnp.einsum('hbic,hbjc->hbij', left_blocks, windows) * scale
    columns, usable = tap_index(disparity, DISP, RAD)
    taps = jnp.take_along_axis(scores.reshape(row_count, col_count, 2 * DISP), columns, axis=2)
    taps = jnp.where(usable, taps, 0.0).astype(jnp.bfloat16)
    motion_pre = jnp.einsum('hwk,km->hwm', taps.astype(jnp.float32), motion_weight.astype(jnp.float32))
    motion = jax.nn.silu(motion_pre).astype(jnp.bfloat16)
    inputs = jnp.concatenate([hidden, motion], axis=2)
    gates = conv_ref(pad_grid(inputs), gate_weight, row_count, col_count)
    update = jax.nn.sigmoid(gates[..., :HID])
    reset = jax.nn.sigmoid(gates[..., HID:])
    hidden_f = hidden.astype(jnp.float32)
    reset_state = (reset * hidden_f).astype(jnp.bfloat16)
    cand_in = jnp.concatenate([reset_state, motion], axis=2)
    cand = jnp.tanh(conv_ref(pad_grid(cand_in), cand_weight, row_count, col_count))
    new_hidden = ((1.0 - update) * hidden_f + update * cand).astype(jnp.bfloat16)
    cotangent = grad_hidden.astype(jnp.float32)
    cand_grad = (cotangent * update * (1.0 - cand * cand)).astype(jnp.bfloat16)
    update_grad = cotangent * (cand - hidden_f) * update * (1.0 - update)
    cand_back = conv_ref(pad_grid(cand_grad), flipped(cand_weight), row_count, col_count)
    reset_grad = cand_back[..., :HID] * hidden_f * reset * (1.0 - reset)
    gate_grads = jnp.concatenate([update_grad, reset_grad], axis=2).astype(jnp.bfloat16)
    gate_back = conv_ref(pad_grid(gate_grads), flipped(gate_weight), row_count, col_count)
    motion_grad = cand_back[..., HID:] + gate_back[..., HID:]
    sigmas = jax.nn.sigmoid(motion_pre)
    pre_grad = (motion_grad * sigmas * (1.0 + motion_pre * (1.0 - sigmas))).astype(jnp.bfloat16)
    tap_grad = jnp.einsum('hwm,km->hwk', pre_grad.astype(jnp.float32), motion_weight.astype(jnp.float32))
    tap_grad = jnp.where(usable, tap_grad, 0.0)
    positions = jnp.arange(2 * DISP, dtype=jnp.int32)
    score_grad = jnp.zeros((row_count, col_count, 2 * DISP), jnp.float32)
    for tap in range(2 * RAD + 1):
        score_grad = score_grad + jnp.where(columns[:, :, tap:tap + 1] == positions, tap_grad[:, :, tap:tap + 1], 0.0)
    score_grad = score_grad.astype(jnp.bfloat16).reshape(row_count, block_count, DISP, 2 * DISP).astype(jnp.float32)
    grad_left = (jnp.einsum('hbij,hbjc->hbic', score_grad, windows) * scale).reshape(row_count, col_count, chan_count).astype(jnp.bfloat16)
    window_grad = jnp.einsum('hbij,hbic->hbjc', score_grad, left_blocks) * scale
    far_part = lax.optimization_barrier(window_grad[:, :, :DISP].astype(jnp.bfloat16)).astype(jnp.float32)
    zero_block = jnp.zeros((row_count, 1, DISP, chan_count), jnp.float32)
    ext_grad = jnp.concatenate([far_part, zero_block], axis=1) + jnp.concatenate([zero_block, window_grad[:, :, DISP:]], axis=1)
    grad_right = ext_grad.reshape(row_count, (block_count + 1) * DISP, chan_count)[:, DISP:].astype(jnp.bfloat16)
    return (new_hidden, grad_left, grad_right)
```

```python
import functools
import math

import jax
import jax.numpy as jnp
from jax import lax
from jax.experimental import pallas as pl
from jax.experimental.pallas import tpu as pltpu
from jax.sharding import PartitionSpec as P

MESH = pl.DeviceIdType.MESH
F32 = jnp.float32
BF = jnp.bfloat16
BAND = 128
ROWS = 16
COLS = 256
WIDE = COLS + 16
HALO = 4
EXT = ROWS + 2 * HALO
CH = 128
CHUNK = 4
N_CHUNK = ROWS // CHUNK


def mm(a, b):
    return jnp.dot(a, b, preferred_element_type=F32)


def mm_nt(a, b):
    return lax.dot_general(a, b, (((1,), (1,)), ((), ())), preferred_element_type=F32)


def mm_tn(a, b):
    return lax.dot_general(a, b, (((0,), (0,)), ((), ())), preferred_element_type=F32)


def sig(v):
    return 0.5 * jnp.tanh(0.5 * v) + 0.5


def put3(ref, row, part, stride, val, forward):
    low = pltpu.roll(val, 1, 0)
    high = pltpu.roll(val, WIDE - 1, 0)
    order = (low, val, high) if forward else (high, val, low)
    for b in range(3):
        at = b * stride + part * CH
        ref[row, :, at : at + CH] = order[b].astype(BF)


def take(values, index):
    return jnp.take_along_axis(values, index, axis=1, mode="promise_in_bounds")


def kernel(
    n_rows, n_cols, taps, scale,
    fl_hbm, fr_hbm, hid_hbm, g_hbm, wg_hbm, wc_hbm, disp, mwp,
    nh, gl, gr,
    fl, fr, prev, far_out, far_in, near1, tap_near,
    hb, gb, mb, in3, ci3, cg3, upd, rst, mpre, cbm,
    wg, wc, wcp, wct, wgp, edge_lo, edge_hi,
    local, send, recv,
):
    rid = lax.axis_index("rows")
    cid = lax.axis_index("cols")
    radius = taps // 2

    has = {
        ("rows", -1): rid > 0,
        ("rows", 1): rid < n_rows - 1,
        ("cols", -1): cid > 0,
        ("cols", 1): cid < n_cols - 1,
    }

    def target(axis, step):
        return (rid + step, cid) if axis == "rows" else (rid, cid + step)

    def message(n, src, dst, axis, step):
        return pltpu.make_async_remote_copy(
            src_ref=src, dst_ref=dst, send_sem=send.at[n], recv_sem=recv.at[n],
            device_id=target(axis, step), device_id_type=MESH,
        )

    def start(spec):
        @pl.when(has[spec[3], spec[4]])
        def _():
            message(*spec).start()

    def finish_send(spec):
        @pl.when(has[spec[3], spec[4]])
        def _():
            message(*spec).wait_send()

    def finish_recv(spec):
        @pl.when(has[spec[3], -spec[4]])
        def _():
            message(*spec).wait_recv()

    own = pl.ds(HALO, ROWS)
    main = pl.ds(0, COLS)
    copies = [
        pltpu.make_async_copy(src, dst, local.at[n])
        for n, (src, dst) in enumerate(
            [
                (fl_hbm, fl),
                (fr_hbm, fr),
                (hid_hbm, hb.at[own, main]),
                (g_hbm, gb.at[own, main]),
                (wg_hbm, wg),
                (wc_hbm, wc),
            ]
        )
    ]
    for copy in copies:
        copy.start()

    barrier = pltpu.get_barrier_semaphore()
    for (axis, step), there in has.items():
        @pl.when(there)
        def _(axis=axis, step=step):
            pl.semaphore_signal(barrier, inc=1, device_id=target(axis, step), device_id_type=MESH)
    peers = sum(there.astype(jnp.int32) for there in has.values())
    pl.semaphore_wait(barrier, peers)

    last = pl.ds(COLS - 16, 16)
    first = pl.ds(0, 16)
    col_msgs = [
        (0, hid_hbm.at[:, last], edge_lo.at[0], "cols", 1),
        (1, hid_hbm.at[:, first], edge_hi.at[0], "cols", -1),
        (2, g_hbm.at[:, last], edge_lo.at[1], "cols", 1),
        (3, g_hbm.at[:, first], edge_hi.at[1], "cols", -1),
    ]
    block_msgs = [
        (
            4 + n,
            fr_hbm.at[pl.ds(n * CHUNK, CHUNK), pl.ds(COLS - BAND, BAND)],
            prev.at[pl.ds(n * CHUNK, CHUNK)],
            "cols",
            1,
        )
        for n in range(N_CHUNK)
    ]
    for spec in col_msgs + block_msgs:
        start(spec)

    def row_msgs(n, buf):
        return [
            (n, buf.at[pl.ds(HALO, HALO)], buf.at[pl.ds(HALO + ROWS, HALO)], "rows", -1),
            (n + 1, buf.at[pl.ds(ROWS, HALO)], buf.at[pl.ds(0, HALO)], "rows", 1),
        ]

    hid_rows, g_rows = row_msgs(8, hb), row_msgs(10, gb)
    motion_cols = [
        (12, mb.at[own, last], edge_lo.at[2], "cols", 1),
        (13, mb.at[own, first], edge_hi.at[2], "cols", -1),
    ]
    motion_rows = row_msgs(14, mb)
    far_msgs = [
        (
            16 + n,
            far_out.at[pl.ds(n * CHUNK, CHUNK)],
            far_in.at[pl.ds(n * CHUNK, CHUNK)],
            "cols",
            -1,
        )
        for n in range(N_CHUNK)
    ]

    @pl.when(jnp.logical_not(has["cols", -1]))
    def _():
        edge_lo[...] = jnp.zeros_like(edge_lo)
        prev[...] = jnp.zeros_like(prev)

    @pl.when(jnp.logical_not(has["cols", 1]))
    def _():
        edge_hi[...] = jnp.zeros_like(edge_hi)
        far_in[...] = jnp.zeros_like(far_in)

    @pl.when(jnp.logical_not(has["rows", -1]))
    def _():
        for buf in (hb, gb, mb):
            buf[0:HALO] = jnp.zeros((HALO, WIDE, CH), BF)

    @pl.when(jnp.logical_not(has["rows", 1]))
    def _():
        for buf in (hb, gb, mb):
            buf[HALO + ROWS : EXT] = jnp.zeros((HALO, WIDE, CH), BF)

    side = lax.broadcasted_iota(jnp.int32, (16, CH), 0) < 8

    def join_edges(which, buf):
        def one(r, carry):
            hi = edge_hi[which, r].astype(F32)
            lo = edge_lo[which, r].astype(F32)
            buf[HALO + r, COLS:WIDE, :] = jnp.where(side, hi, lo).astype(BF)
            return carry

        lax.fori_loop(0, ROWS, one, 0)

    for copy in copies:
        copy.wait()
    for spec in col_msgs:
        finish_recv(spec)
    join_edges(0, hb)
    join_edges(1, gb)
    for spec in hid_rows + g_rows:
        start(spec)

    wcp[...] = jnp.zeros_like(wcp)
    wgp[...] = jnp.zeros_like(wgp)
    for a in range(3):
        for b in range(3):
            t = a * 3 + b
            blk = wc[t * 256 : (t + 1) * 256, :]
            wcp[a * 768 + b * 256 : a * 768 + (b + 1) * 256, 0:CH] = blk
            wcp[(a + 1) * 768 + b * 256 : (a + 1) * 768 + (b + 1) * 256, CH : 2 * CH] = blk
            wct[t * CH : (t + 1) * CH, :] = blk.astype(F32).T.astype(BF)
            turned = wg[t * 256 + CH : (t + 1) * 256, :].astype(F32).T.astype(BF)
            q = 2 - a
            wgp[q * 768 + b * 256 : q * 768 + (b + 1) * 256, 0:CH] = turned
            wgp[(q + 1) * 768 + b * 256 : (q + 1) * 768 + (b + 1) * 256, CH : 2 * CH] = turned

    sub = lax.broadcasted_iota(jnp.int32, (BAND, BAND), 0)
    lane = lax.broadcasted_iota(jnp.int32, (BAND, BAND), 1)
    ones = jnp.ones((BAND, BAND), BF)

    def spread(r, b):
        line = disp[r, :, b * BAND : (b + 1) * BAND].astype(F32)
        diag = jnp.where(sub == lane, line, 0.0).astype(BF)
        return mm(diag, ones).astype(jnp.int32)

    def usable_of(levels0):
        level = levels0 + lane - radius
        return (level >= 0) & (level < BAND) & (lane < taps)

    def clip(v):
        return jnp.clip(v, 0, BAND - 1)

    def finish_motion(r, b, tap):
        pre = mm(tap.astype(BF), mwp[...])
        mpre[r, b * BAND : (b + 1) * BAND, :] = pre
        mb[HALO + r, b * BAND : (b + 1) * BAND, :] = (pre * sig(pre)).astype(BF)

    def near_row(r, carry):
        l0, l1 = fl[r, 0:BAND, :], fl[r, BAND:COLS, :]
        r0, r1 = fr[r, 0:BAND, :], fr[r, BAND:COLS, :]
        d0, d1 = spread(r, 0), spread(r, 1)
        c0 = sub + radius - d0 - lane
        tap_near[r] = jnp.where((c0 >= 0) & usable_of(d0), take(mm_nt(l0, r0) * scale, clip(c0)), 0.0)
        c1 = sub + radius - d1 - lane
        near = take(mm_nt(l1, r1) * scale, clip(c1))
        far = take(mm_nt(l1, r0) * scale, clip(c1 + BAND))
        finish_motion(r, 1, jnp.where(usable_of(d1), jnp.where(c1 >= 0, near, far), 0.0))
        return carry

    lax.fori_loop(0, ROWS, near_row, 0)

    for spec in hid_rows + g_rows:
        finish_recv(spec)

    def fill_hidden(r, carry):
        put3(in3, r, 0, 256, hb[r].astype(F32), True)
        return carry

    lax.fori_loop(0, EXT, fill_hidden, 0)

    def far_row(r, carry):
        d0 = spread(r, 0)
        c0 = sub + radius - d0 - lane
        far = take(mm_nt(fl[r, 0:BAND, :], prev[r]) * scale, clip(c0 + BAND))
        finish_motion(r, 0, jnp.where((c0 < 0) & usable_of(d0), far, tap_near[r]))
        return carry

    for n in range(N_CHUNK):
        finish_recv(block_msgs[n])
        lax.fori_loop(n * CHUNK, (n + 1) * CHUNK, far_row, 0)

    for spec in motion_cols:
        start(spec)
    for spec in motion_cols:
        finish_recv(spec)
    join_edges(2, mb)
    for spec in motion_rows:
        start(spec)

    def fill_motion(r, carry):
        m = mb[r].astype(F32)
        put3(in3, r, 1, 256, m, True)

        @pl.when((r >= 1) & (r < EXT - 1))
        def _():
            put3(ci3, r - 1, 1, 256, m, True)

        return carry

    def gate_row(r, carry):
        acc = mm(in3[r - 1], wg[0:768, :])
        acc = acc + mm(in3[r], wg[768:1536, :])
        acc = acc + mm(in3[r + 1], wg[1536:2304, :])
        reset = sig(acc[:, CH:])
        upd[r - 1] = sig(acc[:, :CH])
        rst[r - 1] = reset
        put3(ci3, r - 1, 0, 256, reset * hb[r].astype(F32), True)
        return carry

    lax.fori_loop(HALO, HALO + ROWS, fill_motion, 0)
    lax.fori_loop(HALO + 1, HALO + ROWS - 1, gate_row, 0)
    for spec in motion_rows:
        finish_recv(spec)
    lax.fori_loop(0, HALO, fill_motion, 0)
    lax.fori_loop(HALO + ROWS, EXT, fill_motion, 0)
    lax.fori_loop(1, HALO + 1, gate_row, 0)
    lax.fori_loop(HALO + ROWS - 1, EXT - 1, gate_row, 0)

    def cand_pair(r, inside):
        acc = mm(ci3[r - 2], wcp[0:768, :])
        for q in range(1, 4):
            acc = acc + mm(ci3[r - 2 + q], wcp[q * 768 : (q + 1) * 768, :])
        for s in range(2):
            c = jnp.tanh(acc[:, s * CH : (s + 1) * CH])
            u = upd[r + s - 1]
            h = hb[r + s].astype(F32)
            g = gb[r + s].astype(F32)
            if inside:
                nh[r + s - HALO] = ((1.0 - u) * h + u * c)[:COLS].astype(BF)
            put3(cg3, r + s - 2, 0, CH, g * u * (1.0 - c * c), False)
            put3(in3, r + s, 0, 256, g * (c - h) * u * (1.0 - u), False)

    def cand_inside(n, carry):
        cand_pair(HALO + 2 * n, True)
        return carry

    cand_pair(2, False)
    lax.fori_loop(0, ROWS // 2, cand_inside, 0)
    cand_pair(HALO + ROWS, False)

    def back_row(r, carry):
        acc = mm(cg3[r - 1], wct[0:384, :])
        acc = acc + mm(cg3[r - 2], wct[384:768, :])
        acc = acc + mm(cg3[r - 3], wct[768:1152, :])
        reset = rst[r - 1]
        grad = acc[:, :CH] * hb[r].astype(F32) * reset * (1.0 - reset)
        put3(in3, r, 1, 256, grad, False)
        cbm[r - 3] = acc[:, CH:]
        return carry

    lax.fori_loop(HALO - 1, HALO + ROWS + 1, back_row, 0)

    def tail_row(r, motion_grad):
        pre = mpre[r]
        s = sig(pre)
        pre_grad = (motion_grad * s * (1.0 + pre * (1.0 - s))).astype(BF)
        parts = []
        for b in range(2):
            d = spread(r, b)
            tap = mm_nt(pre_grad[b * BAND : (b + 1) * BAND, :], mwp[...])
            tap = jnp.where(usable_of(d), tap, 0.0)
            k = sub + radius - d - lane
            g_near = jnp.where(k >= 0, take(tap, clip(k)), 0.0).astype(BF)
            g_far = jnp.where(k + BAND >= 0, take(tap, clip(k + BAND)), 0.0).astype(BF)
            lb = fl[r, b * BAND : (b + 1) * BAND, :]
            rb = fr[r, b * BAND : (b + 1) * BAND, :]
            pb = prev[r] if b == 0 else fr[r, 0:BAND, :]
            gl[r, b * BAND : (b + 1) * BAND, :] = ((mm(g_near, rb) + mm(g_far, pb)) * scale).astype(BF)
            parts.append((mm_tn(g_near, lb) * scale, (mm_tn(g_far, lb) * scale).astype(BF)))
        far_out[r] = parts[0][1]
        gr[r, 0:BAND, :] = (parts[0][0] + parts[1][1].astype(F32)).astype(BF)
        near1[r] = parts[1][0]

    def tail_pair(n, carry):
        r = HALO + 2 * n
        acc = mm(in3[r - 1, 0:COLS], wgp[0:768, :])
        for q in range(1, 4):
            acc = acc + mm(in3[r - 1 + q, 0:COLS], wgp[q * 768 : (q + 1) * 768, :])
        for s in range(2):
            tail_row(2 * n + s, acc[:, s * CH : (s + 1) * CH] + cbm[r + s - 3, 0:COLS])
        return carry

    for n in range(N_CHUNK):
        lax.fori_loop(n * (CHUNK // 2), (n + 1) * (CHUNK // 2), tail_pair, 0)
        start(far_msgs[n])

    def add_far(r, carry):
        gr[r, BAND:COLS, :] = (near1[r] + far_in[r].astype(F32)).astype(BF)
        return carry

    for n in range(N_CHUNK):
        finish_recv(far_msgs[n])
        lax.fori_loop(n * CHUNK, (n + 1) * CHUNK, add_far, 0)
    for spec in col_msgs + block_msgs + hid_rows + g_rows + motion_cols + motion_rows + far_msgs:
        finish_send(spec)


def per_device(n_rows, n_cols, feat_left, feat_right, hidden, disparity, motion_weight, gate_weight, cand_weight, grad_hidden):
    taps = motion_weight.shape[0]
    feat = feat_left.shape[2]
    mwp = jnp.pad(motion_weight, ((0, BAND - taps), (0, 0)))
    wg = gate_weight.reshape(9 * 256, 256)
    wc = cand_weight.reshape(9 * 256, CH)
    hbm = pl.BlockSpec(memory_space=pl.ANY)
    vmem = pl.BlockSpec(memory_space=pltpu.VMEM)
    v = pltpu.VMEM
    return pl.pallas_call(
        functools.partial(kernel, n_rows, n_cols, taps, 1.0 / math.sqrt(feat)),
        out_shape=(
            jax.ShapeDtypeStruct(hidden.shape, BF),
            jax.ShapeDtypeStruct(feat_left.shape, BF),
            jax.ShapeDtypeStruct(feat_right.shape, BF),
        ),
        in_specs=[hbm] * 6 + [vmem] * 2,
        out_specs=(vmem,) * 3,
        scratch_shapes=[
            v((ROWS, COLS, feat), BF),
            v((ROWS, COLS, feat), BF),
            v((ROWS, BAND, feat), BF),
            v((ROWS, BAND, feat), BF),
            v((ROWS, BAND, feat), BF),
            v((ROWS, BAND, feat), F32),
            v((ROWS, BAND, BAND), F32),
            v((EXT, WIDE, CH), BF),
            v((EXT, WIDE, CH), BF),
            v((EXT, WIDE, CH), BF),
            v((EXT, WIDE, 6 * CH), BF),
            v((EXT - 2, WIDE, 6 * CH), BF),
            v((EXT - 4, WIDE, 3 * CH), BF),
            v((EXT - 2, WIDE, CH), F32),
            v((EXT - 2, WIDE, CH), F32),
            v((ROWS, COLS, CH), F32),
            v((ROWS + 2, WIDE, CH), F32),
            v((9 * 256, 256), BF),
            v((9 * 256, CH), BF),
            v((12 * 256, 256), BF),
            v((9 * CH, 256), BF),
            v((12 * 256, 256), BF),
            v((3, ROWS, 16, CH), BF),
            v((3, ROWS, 16, CH), BF),
            pltpu.SemaphoreType.DMA((6,)),
            pltpu.SemaphoreType.DMA((16 + N_CHUNK,)),
            pltpu.SemaphoreType.DMA((16 + N_CHUNK,)),
        ],
        compiler_params=pltpu.CompilerParams(
            collective_id=0, has_side_effects=True, vmem_limit_bytes=63 * 1024 * 1024
        ),
        cost_estimate=pl.CostEstimate(flops=17 * 10**9, bytes_accessed=14 * 10**6, transcendentals=0),
    )(feat_left, feat_right, hidden, grad_hidden, wg, wc, disparity[:, None, :], mwp)


def solution(mesh):
    blocks = P("rows", "cols", None)
    return jax.shard_map(
        functools.partial(per_device, mesh.shape["rows"], mesh.shape["cols"]),
        mesh=mesh,
        in_specs=(blocks, blocks, blocks, P("rows", "cols"), P(), P(), P(), blocks),
        out_specs=(blocks, blocks, blocks),
        check_vma=False,
    )
```

```python
import functools
import math

import jax
import jax.numpy as jnp
from jax import lax
from jax.experimental import pallas as pl
from jax.experimental.pallas import tpu as pltpu
from jax.sharding import PartitionSpec as P

MESH = pl.DeviceIdType.MESH
F32 = jnp.float32
BF = jnp.bfloat16
BAND = 128
ROWS = 16
COLS = 256
WIDE = COLS + 16
HALO = 4
EXT = ROWS + 2 * HALO
CH = 128
FWD = 9
BWD = ROWS - FWD
TAP_PAD = 16
FWD_CHUNKS = ((0, 3), (3, 3), (6, 3))
BWD_CHUNKS = ((0, 4), (4, 3))
N_MSG = 17 + 2 * len(FWD_CHUNKS) + 4 * len(BWD_CHUNKS)


def mm(a, b):
    return jnp.dot(a, b, preferred_element_type=F32)


def mm_nt(a, b):
    return lax.dot_general(a, b, (((1,), (1,)), ((), ())), preferred_element_type=F32)


def mm_tn(a, b):
    return lax.dot_general(a, b, (((0,), (0,)), ((), ())), preferred_element_type=F32)


def sig(v):
    return 0.5 * jnp.tanh(0.5 * v) + 0.5


def put3(ref, row, part, stride, val, forward):
    low = pltpu.roll(val, 1, 0)
    high = pltpu.roll(val, WIDE - 1, 0)
    order = (low, val, high) if forward else (high, val, low)
    for b in range(3):
        at = b * stride + part * CH
        ref[row, :, at : at + CH] = order[b].astype(BF)


def take(values, index):
    return jnp.take_along_axis(values, index, axis=1, mode="promise_in_bounds")


def kernel(
    n_rows, n_cols, taps, scale,
    fl_hbm, fr_hbm, hid_hbm, g_hbm, wg_hbm, wc_hbm, disp_in, mw,
    nh, gl, gr,
    fl, fr, prev, left_in, disp_next, far_out, far_in, part_out, part_in, tap_out, tap_in,
    near1, tap_near, disp, mwp,
    hb, gb, mb, in3, ci3, cg3, upd, rst, mpre, cbm,
    wg, wc, wcp, wct, wgp, edge_lo, edge_hi,
    local, send, recv,
):
    rid = lax.axis_index("rows")
    cid = lax.axis_index("cols")
    radius = taps // 2

    has = {
        ("rows", -1): rid > 0,
        ("rows", 1): rid < n_rows - 1,
        ("cols", -1): cid > 0,
        ("cols", 1): cid < n_cols - 1,
    }

    def target(axis, step):
        return (rid + step, cid) if axis == "rows" else (rid, cid + step)

    def message(n, src, dst, axis, step):
        return pltpu.make_async_remote_copy(
            src_ref=src, dst_ref=dst, send_sem=send.at[n], recv_sem=recv.at[n],
            device_id=target(axis, step), device_id_type=MESH,
        )

    def start(spec):
        @pl.when(has[spec[3], spec[4]])
        def _():
            message(*spec).start()

    def finish_send(spec):
        @pl.when(has[spec[3], spec[4]])
        def _():
            message(*spec).wait_send()

    def finish_recv(spec):
        @pl.when(has[spec[3], -spec[4]])
        def _():
            message(*spec).wait_recv()

    own = pl.ds(HALO, ROWS)
    main = pl.ds(0, COLS)
    copies = [
        pltpu.make_async_copy(src, dst, local.at[n])
        for n, (src, dst) in enumerate(
            [
                (fl_hbm, fl),
                (fr_hbm, fr),
                (hid_hbm, hb.at[own, main]),
                (g_hbm, gb.at[own, main]),
                (wg_hbm, wg),
                (wc_hbm, wc),
            ]
        )
    ]
    for copy in copies:
        copy.start()

    barrier = pltpu.get_barrier_semaphore()
    for (axis, step), there in has.items():
        @pl.when(there)
        def _(axis=axis, step=step):
            pl.semaphore_signal(barrier, inc=1, device_id=target(axis, step), device_id_type=MESH)
    peers = sum(there.astype(jnp.int32) for there in has.values())
    pl.semaphore_wait(barrier, peers)

    last = pl.ds(COLS - 16, 16)
    first = pl.ds(0, 16)
    col_msgs = [
        (0, hid_hbm.at[:, last], edge_lo.at[0], "cols", 1),
        (1, hid_hbm.at[:, first], edge_hi.at[0], "cols", -1),
        (2, g_hbm.at[:, last], edge_lo.at[1], "cols", 1),
        (3, g_hbm.at[:, first], edge_hi.at[1], "cols", -1),
    ]
    bands = pl.ds(0, BAND)
    tail_band = pl.ds(COLS - BAND, BAND)
    base = 17
    right_msgs, left_msgs, tap_msgs, slope_msgs, far_msgs, part_msgs = [], [], [], [], [], []
    for at, size in FWD_CHUNKS:
        rows = pl.ds(at, size)
        right_msgs.append((base, fr_hbm.at[rows, tail_band], prev.at[rows], "cols", 1))
        far_msgs.append((base + 1, far_out.at[rows], far_in.at[rows], "cols", -1))
        base += 2
    for at, size in BWD_CHUNKS:
        rows, whole = pl.ds(at, size), pl.ds(FWD + at, size)
        left_msgs.append((base, fl_hbm.at[whole, bands], left_in.at[rows], "cols", -1))
        tap_msgs.append((base + 1, tap_out.at[0, rows], tap_in.at[0, rows], "cols", 1))
        slope_msgs.append((base + 2, tap_out.at[1, rows], tap_in.at[1, rows], "cols", -1))
        part_msgs.append((base + 3, part_out.at[rows], part_in.at[rows], "cols", 1))
        base += 4
    disp_msg = (16, disp.at[pl.ds(FWD, BWD)], disp_next, "cols", -1)
    for r in range(ROWS):
        disp[r] = disp_in[r : r + 1, :]
    for spec in col_msgs + [disp_msg] + left_msgs + right_msgs:
        start(spec)
    mwp[...] = jnp.zeros_like(mwp)
    mwp[0:taps, :] = mw[...]

    def row_msgs(n, buf):
        return [
            (n, buf.at[pl.ds(HALO, HALO)], buf.at[pl.ds(HALO + ROWS, HALO)], "rows", -1),
            (n + 1, buf.at[pl.ds(ROWS, HALO)], buf.at[pl.ds(0, HALO)], "rows", 1),
        ]

    hid_rows, g_rows = row_msgs(8, hb), row_msgs(10, gb)
    motion_cols = [
        (12, mb.at[own, last], edge_lo.at[2], "cols", 1),
        (13, mb.at[own, first], edge_hi.at[2], "cols", -1),
    ]
    motion_rows = row_msgs(14, mb)
    @pl.when(jnp.logical_not(has["cols", -1]))
    def _():
        edge_lo[...] = jnp.zeros_like(edge_lo)
        prev[...] = jnp.zeros_like(prev)
        tap_in[0] = jnp.zeros(tap_in.shape[1:], BF)
        part_in[...] = jnp.zeros_like(part_in)

    @pl.when(jnp.logical_not(has["cols", 1]))
    def _():
        edge_hi[...] = jnp.zeros_like(edge_hi)
        far_in[...] = jnp.zeros_like(far_in)
        left_in[...] = jnp.zeros_like(left_in)
        disp_next[...] = jnp.zeros_like(disp_next)
        tap_in[1] = jnp.zeros(tap_in.shape[1:], BF)

    @pl.when(jnp.logical_not(has["rows", -1]))
    def _():
        for buf in (hb, gb, mb):
            buf[0:HALO] = jnp.zeros((HALO, WIDE, CH), BF)

    @pl.when(jnp.logical_not(has["rows", 1]))
    def _():
        for buf in (hb, gb, mb):
            buf[HALO + ROWS : EXT] = jnp.zeros((HALO, WIDE, CH), BF)

    side = lax.broadcasted_iota(jnp.int32, (16, CH), 0) < 8

    def join_edges(which, buf):
        def one(r, carry):
            hi = edge_hi[which, r].astype(F32)
            lo = edge_lo[which, r].astype(F32)
            buf[HALO + r, COLS:WIDE, :] = jnp.where(side, hi, lo).astype(BF)
            return carry

        lax.fori_loop(0, ROWS, one, 0)

    for copy in copies:
        copy.wait()
    for spec in col_msgs:
        finish_recv(spec)
    join_edges(0, hb)
    join_edges(1, gb)
    for spec in hid_rows + g_rows:
        start(spec)

    wcp[...] = jnp.zeros_like(wcp)
    wgp[...] = jnp.zeros_like(wgp)
    for a in range(3):
        for b in range(3):
            t = a * 3 + b
            blk = wc[t * 256 : (t + 1) * 256, :]
            wcp[a * 768 + b * 256 : a * 768 + (b + 1) * 256, 0:CH] = blk
            wcp[(a + 1) * 768 + b * 256 : (a + 1) * 768 + (b + 1) * 256, CH : 2 * CH] = blk
            wct[t * CH : (t + 1) * CH, :] = blk.astype(F32).T.astype(BF)
            turned = wg[t * 256 + CH : (t + 1) * 256, :].astype(F32).T.astype(BF)
            q = 2 - a
            wgp[q * 768 + b * 256 : q * 768 + (b + 1) * 256, 0:CH] = turned
            wgp[(q + 1) * 768 + b * 256 : (q + 1) * 768 + (b + 1) * 256, CH : 2 * CH] = turned

    sub = lax.broadcasted_iota(jnp.int32, (BAND, BAND), 0)
    lane = lax.broadcasted_iota(jnp.int32, (BAND, BAND), 1)
    ones = jnp.ones((BAND, BAND), BF)

    turn = (lax.broadcasted_iota(jnp.int32, (TAP_PAD, BAND), 0) == lax.broadcasted_iota(jnp.int32, (TAP_PAD, BAND), 1)).astype(BF)
    back = (sub == lane).astype(BF)[0:TAP_PAD]

    def spread_line(line):
        diag = jnp.where(sub == lane, line.astype(F32), 0.0).astype(BF)
        return mm(diag, ones).astype(jnp.int32)

    def spread(r, b):
        return spread_line(disp[r, :, b * BAND : (b + 1) * BAND])

    def usable_of(levels0):
        level = levels0 + lane - radius
        return (level >= 0) & (level < BAND) & (lane < taps)

    def clip(v):
        return jnp.clip(v, 0, BAND - 1)

    def finish_motion(r, b, pre):
        mpre[r, b * BAND : (b + 1) * BAND, :] = pre
        mb[HALO + r, b * BAND : (b + 1) * BAND, :] = (pre * sig(pre)).astype(BF)

    def near_row(r, carry):
        l0, l1 = fl[r, 0:BAND, :], fl[r, BAND:COLS, :]
        r0, r1 = fr[r, 0:BAND, :], fr[r, BAND:COLS, :]
        d0, d1 = spread(r, 0), spread(r, 1)
        c0 = sub + radius - d0 - lane
        tap_near[r] = jnp.where((c0 >= 0) & usable_of(d0), take(mm_nt(l0, r0) * scale, clip(c0)), 0.0)
        c1 = sub + radius - d1 - lane
        near = take(mm_nt(l1, r1) * scale, clip(c1))
        far = take(mm_nt(l1, r0) * scale, clip(c1 + BAND))
        tap = jnp.where(usable_of(d1), jnp.where(c1 >= 0, near, far), 0.0)
        finish_motion(r, 1, mm(tap.astype(BF), mwp[...]))
        return carry

    lax.fori_loop(0, ROWS, near_row, 0)
    start(motion_cols[0])

    for spec in hid_rows + g_rows:
        finish_recv(spec)

    def fill_hidden(r, carry):
        put3(in3, r, 0, 256, hb[r].astype(F32), True)
        return carry

    lax.fori_loop(0, EXT, fill_hidden, 0)

    def far_row(r, carry):
        d0 = spread(r, 0)
        c0 = sub + radius - d0 - lane
        far = take(mm_nt(fl[r, 0:BAND, :], prev[r]) * scale, clip(c0 + BAND))
        tap = jnp.where((c0 < 0) & usable_of(d0), far, tap_near[r])
        finish_motion(r, 0, mm(tap.astype(BF), mwp[...]))
        return carry

    def next_row(i, carry):
        d = spread_line(disp_next[i, :, 0:BAND])
        c = sub + radius - d - lane
        far = take(mm_nt(left_in[i], fr[FWD + i, BAND:COLS, :]) * scale, clip(c + BAND))
        tap = jnp.where((c < 0) & usable_of(d), far, 0.0).astype(BF)
        tap_out[0, i] = mm_nt(turn, tap).astype(BF)
        return carry

    def taken_row(i, carry):
        pre = mm(tap_near[FWD + i].astype(BF), mwp[...])
        finish_motion(FWD + i, 0, pre + mm_tn(tap_in[0, i], mwp[0:TAP_PAD, :]))
        return carry

    def over(chunk, body):
        lax.fori_loop(chunk[0], chunk[0] + chunk[1], body, 0)

    finish_recv(disp_msg)
    for n, chunk in enumerate(BWD_CHUNKS):
        finish_recv(right_msgs[n])
        over(FWD_CHUNKS[n], far_row)
        finish_recv(left_msgs[n])
        over(chunk, next_row)
        start(tap_msgs[n])
    for n in range(len(BWD_CHUNKS), len(FWD_CHUNKS)):
        finish_recv(right_msgs[n])
        over(FWD_CHUNKS[n], far_row)
    for n, chunk in enumerate(BWD_CHUNKS):
        finish_recv(tap_msgs[n])
        over(chunk, taken_row)

    start(motion_cols[1])
    for spec in motion_cols:
        finish_recv(spec)
    join_edges(2, mb)
    for spec in motion_rows:
        start(spec)

    def fill_motion(r, carry):
        m = mb[r].astype(F32)
        put3(in3, r, 1, 256, m, True)

        @pl.when((r >= 1) & (r < EXT - 1))
        def _():
            put3(ci3, r - 1, 1, 256, m, True)

        return carry

    def gate_row(r, carry):
        acc = mm(in3[r - 1], wg[0:768, :])
        acc = acc + mm(in3[r], wg[768:1536, :])
        acc = acc + mm(in3[r + 1], wg[1536:2304, :])
        reset = sig(acc[:, CH:])
        upd[r - 1] = sig(acc[:, :CH])
        rst[r - 1] = reset
        put3(ci3, r - 1, 0, 256, reset * hb[r].astype(F32), True)
        return carry

    lax.fori_loop(HALO, HALO + ROWS, fill_motion, 0)
    lax.fori_loop(HALO + 1, HALO + ROWS - 1, gate_row, 0)
    for spec in motion_rows:
        finish_recv(spec)
    lax.fori_loop(0, HALO, fill_motion, 0)
    lax.fori_loop(HALO + ROWS, EXT, fill_motion, 0)
    lax.fori_loop(1, HALO + 1, gate_row, 0)
    lax.fori_loop(HALO + ROWS - 1, EXT - 1, gate_row, 0)

    def cand_pair(r, inside):
        acc = mm(ci3[r - 2], wcp[0:768, :])
        for q in range(1, 4):
            acc = acc + mm(ci3[r - 2 + q], wcp[q * 768 : (q + 1) * 768, :])
        for s in range(2):
            c = jnp.tanh(acc[:, s * CH : (s + 1) * CH])
            u = upd[r + s - 1]
            h = hb[r + s].astype(F32)
            g = gb[r + s].astype(F32)
            if inside:
                nh[r + s - HALO] = ((1.0 - u) * h + u * c)[:COLS].astype(BF)
            put3(cg3, r + s - 2, 0, CH, g * u * (1.0 - c * c), False)
            put3(in3, r + s, 0, 256, g * (c - h) * u * (1.0 - u), False)

    def cand_inside(n, carry):
        cand_pair(HALO + 2 * n, True)
        return carry

    cand_pair(2, False)
    lax.fori_loop(0, ROWS // 2, cand_inside, 0)
    cand_pair(HALO + ROWS, False)

    def back_row(r, carry):
        acc = mm(cg3[r - 1], wct[0:384, :])
        acc = acc + mm(cg3[r - 2], wct[384:768, :])
        acc = acc + mm(cg3[r - 3], wct[768:1152, :])
        reset = rst[r - 1]
        grad = acc[:, :CH] * hb[r].astype(F32) * reset * (1.0 - reset)
        put3(in3, r, 1, 256, grad, False)
        cbm[r - 3] = acc[:, CH:]
        return carry

    lax.fori_loop(HALO - 1, HALO + ROWS + 1, back_row, 0)

    def slopes(n, b, store):
        r = HALO + 4 * n
        cut = slice(b * BAND, (b + 1) * BAND)
        acc = None
        for q in range(4):
            lhs = jnp.concatenate([in3[r - 1 + q, cut], in3[r + 1 + q, cut]], axis=0)
            term = mm(lhs, wgp[q * 768 : (q + 1) * 768, :])
            acc = term if acc is None else acc + term
        for s in range(4):
            row = 4 * n + s
            half = acc[(s // 2) * BAND : (s // 2 + 1) * BAND, (s % 2) * CH : (s % 2 + 1) * CH]
            motion_grad = half + cbm[row + 1, cut]
            pre = mpre[row, cut]
            sg = sig(pre)
            pre_grad = (motion_grad * sg * (1.0 + pre * (1.0 - sg))).astype(BF)
            d = spread(row, b)
            tap = jnp.where(usable_of(d), mm_nt(pre_grad, mwp[...]), 0.0)
            store(row, d, tap)

    def g_of(tap, d, shift):
        k = sub + (radius + shift) - d - lane
        return jnp.where(k >= 0, take(tap, clip(k)), 0.0).astype(BF)

    def keep_tap(row, d, tap):
        tap_near[row] = tap

        @pl.when(row >= FWD)
        def _():
            tap_out[1, row - FWD] = mm_nt(turn, tap.astype(BF)).astype(BF)

    def first_slopes(n, carry):
        slopes(n, 0, keep_tap)
        return carry

    def send_far(r, carry):
        g_far = g_of(tap_near[r], spread(r, 0), BAND)
        far_out[r] = (mm_tn(g_far, fl[r, 0:BAND, :]) * scale).astype(BF)
        return carry

    def send_part(i, carry):
        d = spread_line(disp_next[i, :, 0:BAND])
        tap = mm_tn(tap_in[1, i], back)
        g_far = g_of(tap, d, BAND)
        part_out[i] = (mm(g_far, fr[FWD + i, BAND:COLS, :]) * scale).astype(BF)
        near1[FWD + i] = mm_tn(g_far, left_in[i]) * scale
        return carry

    def own_second(row, d, tap):
        g_near, g_far = g_of(tap, d, 0), g_of(tap, d, BAND)
        l0, l1 = fl[row, 0:BAND, :], fl[row, BAND:COLS, :]
        r0, r1 = fr[row, 0:BAND, :], fr[row, BAND:COLS, :]
        gl[row, BAND:COLS, :] = ((mm(g_near, r1) + mm(g_far, r0)) * scale).astype(BF)
        g_first = g_of(tap_near[row], spread(row, 0), 0)
        far = (mm_tn(g_far, l1) * scale).astype(BF).astype(F32)
        gr[row, 0:BAND, :] = (mm_tn(g_first, l0) * scale + far).astype(BF)
        near = mm_tn(g_near, l1) * scale
        first = mm(g_first, r0)

        @pl.when(row < FWD)
        def _():
            g_back = g_of(tap_near[row], spread(row, 0), BAND)
            gl[row, 0:BAND, :] = ((first + mm(g_back, prev[jnp.minimum(row, FWD - 1)])) * scale).astype(BF)
            near1[row] = near

        @pl.when(row >= FWD)
        def _():
            gr[row, BAND:COLS, :] = (near + near1[row].astype(BF).astype(F32)).astype(BF)
            near1[row] = first * scale

    def second_slopes(n, carry):
        slopes(n, 1, own_second)
        return carry

    quads = ROWS // 4
    split = FWD // 4
    lax.fori_loop(split, quads, first_slopes, 0)
    for spec in slope_msgs:
        start(spec)
    lax.fori_loop(0, split, first_slopes, 0)
    for n, chunk in enumerate(FWD_CHUNKS):
        over(chunk, send_far)
        start(far_msgs[n])
    for n, chunk in enumerate(BWD_CHUNKS):
        finish_recv(slope_msgs[n])
        over(chunk, send_part)
        start(part_msgs[n])
    lax.fori_loop(0, quads, second_slopes, 0)

    def add_far(r, carry):
        gr[r, BAND:COLS, :] = (near1[r] + far_in[r].astype(F32)).astype(BF)
        return carry

    def add_part(i, carry):
        gl[FWD + i, 0:BAND, :] = (near1[FWD + i] + part_in[i].astype(F32)).astype(BF)
        return carry

    for n, chunk in enumerate(FWD_CHUNKS):
        finish_recv(far_msgs[n])
        over(chunk, add_far)
    for n, chunk in enumerate(BWD_CHUNKS):
        finish_recv(part_msgs[n])
        over(chunk, add_part)
    sent = col_msgs + [disp_msg] + left_msgs + right_msgs + hid_rows + g_rows + motion_cols + motion_rows
    for spec in sent + tap_msgs + slope_msgs + far_msgs + part_msgs:
        finish_send(spec)


def per_device(n_rows, n_cols, feat_left, feat_right, hidden, disparity, motion_weight, gate_weight, cand_weight, grad_hidden):
    taps = motion_weight.shape[0]
    feat = feat_left.shape[2]
    wg = gate_weight.reshape(9 * 256, 256)
    wc = cand_weight.reshape(9 * 256, CH)
    hbm = pl.BlockSpec(memory_space=pl.ANY)
    vmem = pl.BlockSpec(memory_space=pltpu.VMEM)
    v = pltpu.VMEM
    return pl.pallas_call(
        functools.partial(kernel, n_rows, n_cols, taps, 1.0 / math.sqrt(feat)),
        out_shape=(
            jax.ShapeDtypeStruct(hidden.shape, BF),
            jax.ShapeDtypeStruct(feat_left.shape, BF),
            jax.ShapeDtypeStruct(feat_right.shape, BF),
        ),
        in_specs=[hbm] * 6 + [vmem] * 2,
        out_specs=(vmem,) * 3,
        scratch_shapes=[
            v((ROWS, COLS, feat), BF),
            v((ROWS, COLS, feat), BF),
            v((FWD, BAND, feat), BF),
            v((BWD, BAND, feat), BF),
            v((BWD, 1, COLS), jnp.int32),
            v((FWD, BAND, feat), BF),
            v((FWD, BAND, feat), BF),
            v((BWD, BAND, feat), BF),
            v((BWD, BAND, feat), BF),
            v((2, BWD, TAP_PAD, BAND), BF),
            v((2, BWD, TAP_PAD, BAND), BF),
            v((ROWS, BAND, feat), F32),
            v((ROWS, BAND, BAND), F32),
            v((ROWS, 1, COLS), jnp.int32),
            v((BAND, CH), BF),
            v((EXT, WIDE, CH), BF),
            v((EXT, WIDE, CH), BF),
            v((EXT, WIDE, CH), BF),
            v((EXT, WIDE, 6 * CH), BF),
            v((EXT - 2, WIDE, 6 * CH), BF),
            v((EXT - 4, WIDE, 3 * CH), BF),
            v((EXT - 2, WIDE, CH), F32),
            v((EXT - 2, WIDE, CH), F32),
            v((ROWS, COLS, CH), F32),
            v((ROWS + 2, WIDE, CH), F32),
            v((9 * 256, 256), BF),
            v((9 * 256, CH), BF),
            v((12 * 256, 256), BF),
            v((9 * CH, 256), BF),
            v((12 * 256, 256), BF),
            v((3, ROWS, 16, CH), BF),
            v((3, ROWS, 16, CH), BF),
            pltpu.SemaphoreType.DMA((6,)),
            pltpu.SemaphoreType.DMA((N_MSG,)),
            pltpu.SemaphoreType.DMA((N_MSG,)),
        ],
        compiler_params=pltpu.CompilerParams(
            collective_id=0, has_side_effects=True, vmem_limit_bytes=63 * 1024 * 1024
        ),
        cost_estimate=pl.CostEstimate(flops=17 * 10**9, bytes_accessed=14 * 10**6, transcendentals=0),
    )(feat_left, feat_right, hidden, grad_hidden, wg, wc, disparity, motion_weight)


def solution(mesh):
    blocks = P("rows", "cols", None)
    return jax.shard_map(
        functools.partial(per_device, mesh.shape["rows"], mesh.shape["cols"]),
        mesh=mesh,
        in_specs=(blocks, blocks, blocks, P("rows", "cols"), P(), P(), P(), blocks),
        out_specs=(blocks, blocks, blocks),
        check_vma=False,
    )
```

```python
import functools
import math

import jax
import jax.numpy as jnp
from jax import lax
from jax.experimental import pallas as pl
from jax.experimental.pallas import tpu as pltpu
from jax.sharding import PartitionSpec as P

MESH = pl.DeviceIdType.MESH
F32 = jnp.float32
BF = jnp.bfloat16
BAND = 128
ROWS = 16
COLS = 256
WIDE = COLS + 16
HALO = 4
EXT = ROWS + 2 * HALO
CH = 128
FWD = 9
BWD = ROWS - FWD
TAP_PAD = 16
FWD_CHUNKS = ((0, 3), (3, 3), (6, 3))
BWD_CHUNKS = ((0, 4), (4, 3))
N_MSG = 17 + 2 * len(FWD_CHUNKS) + 4 * len(BWD_CHUNKS)


def mm(a, b):
    return jnp.dot(a, b, preferred_element_type=F32)


def mm_nt(a, b):
    return lax.dot_general(a, b, (((1,), (1,)), ((), ())), preferred_element_type=F32)


def mm_tn(a, b):
    return lax.dot_general(a, b, (((0,), (0,)), ((), ())), preferred_element_type=F32)


def sig(v):
    return 0.5 * jnp.tanh(0.5 * v) + 0.5


def put3(ref, row, part, stride, val, forward):
    low = pltpu.roll(val, 1, 0)
    high = pltpu.roll(val, WIDE - 1, 0)
    order = (low, val, high) if forward else (high, val, low)
    for b in range(3):
        at = b * stride + part * CH
        ref[row, :, at : at + CH] = order[b].astype(BF)


def loop(low, high, body, by):
    whole = (high - low) // by

    def step(n, carry):
        for s in range(by):
            body(low + n * by + s)
        return carry

    if whole > 1:
        lax.fori_loop(0, whole, step, 0)
    elif whole == 1:
        step(0, 0)
    for n in range(low + whole * by, high):
        body(n)


def take(values, index):
    return jnp.take_along_axis(values, index, axis=1, mode="promise_in_bounds")


def kernel(
    n_rows, n_cols, taps, scale,
    fl_hbm, fr_hbm, hid_hbm, g_hbm, wg_hbm, wc_hbm, disp_in, mw,
    nh, gl, gr,
    fl, fr, prev, left_in, disp_next, far_out, far_in, part_out, part_in, tap_out, tap_in,
    near1, tap_near, disp, mwp,
    hb, gb, mb, in3, ci3, cg3, upd, rst, mpre, cbm,
    wg, wc, wcp, wct, wgp, edge_lo, edge_hi,
    local, send, recv,
):
    rid = lax.axis_index("rows")
    cid = lax.axis_index("cols")
    radius = taps // 2

    has = {
        ("rows", -1): rid > 0,
        ("rows", 1): rid < n_rows - 1,
        ("cols", -1): cid > 0,
        ("cols", 1): cid < n_cols - 1,
    }

    def target(axis, step):
        return (rid + step, cid) if axis == "rows" else (rid, cid + step)

    def message(n, src, dst, axis, step):
        return pltpu.make_async_remote_copy(
            src_ref=src, dst_ref=dst, send_sem=send.at[n], recv_sem=recv.at[n],
            device_id=target(axis, step), device_id_type=MESH,
        )

    def start(spec):
        @pl.when(has[spec[3], spec[4]])
        def _():
            message(*spec).start()

    def finish_send(spec):
        @pl.when(has[spec[3], spec[4]])
        def _():
            message(*spec).wait_send()

    def finish_recv(spec):
        @pl.when(has[spec[3], -spec[4]])
        def _():
            message(*spec).wait_recv()

    own = pl.ds(HALO, ROWS)
    main = pl.ds(0, COLS)
    copies = [
        pltpu.make_async_copy(src, dst, local.at[n])
        for n, (src, dst) in enumerate(
            [
                (fl_hbm, fl),
                (fr_hbm, fr),
                (hid_hbm, hb.at[own, main]),
                (g_hbm, gb.at[own, main]),
                (wg_hbm, wg),
                (wc_hbm, wc),
            ]
        )
    ]
    for copy in copies:
        copy.start()

    barrier = pltpu.get_barrier_semaphore()
    for (axis, step), there in has.items():
        @pl.when(there)
        def _(axis=axis, step=step):
            pl.semaphore_signal(barrier, inc=1, device_id=target(axis, step), device_id_type=MESH)
    peers = sum(there.astype(jnp.int32) for there in has.values())
    pl.semaphore_wait(barrier, peers)

    last = pl.ds(COLS - 16, 16)
    first = pl.ds(0, 16)
    col_msgs = [
        (0, hid_hbm.at[:, last], edge_lo.at[0], "cols", 1),
        (1, hid_hbm.at[:, first], edge_hi.at[0], "cols", -1),
        (2, g_hbm.at[:, last], edge_lo.at[1], "cols", 1),
        (3, g_hbm.at[:, first], edge_hi.at[1], "cols", -1),
    ]
    bands = pl.ds(0, BAND)
    tail_band = pl.ds(COLS - BAND, BAND)
    base = 17
    right_msgs, left_msgs, tap_msgs, slope_msgs, far_msgs, part_msgs = [], [], [], [], [], []
    for at, size in FWD_CHUNKS:
        rows = pl.ds(at, size)
        right_msgs.append((base, fr_hbm.at[rows, tail_band], prev.at[rows], "cols", 1))
        far_msgs.append((base + 1, far_out.at[rows], far_in.at[rows], "cols", -1))
        base += 2
    for at, size in BWD_CHUNKS:
        rows, whole = pl.ds(at, size), pl.ds(FWD + at, size)
        left_msgs.append((base, fl_hbm.at[whole, bands], left_in.at[rows], "cols", -1))
        tap_msgs.append((base + 1, tap_out.at[0, rows], tap_in.at[0, rows], "cols", 1))
        slope_msgs.append((base + 2, tap_out.at[1, rows], tap_in.at[1, rows], "cols", -1))
        part_msgs.append((base + 3, part_out.at[rows], part_in.at[rows], "cols", 1))
        base += 4
    disp_msg = (16, disp.at[pl.ds(FWD, BWD)], disp_next, "cols", -1)
    for r in range(ROWS):
        disp[r] = disp_in[r : r + 1, :]
    for spec in col_msgs + [disp_msg] + left_msgs + right_msgs:
        start(spec)
    mwp[...] = jnp.zeros_like(mwp)
    mwp[0:taps, :] = mw[...]

    def row_msgs(n, buf):
        return [
            (n, buf.at[pl.ds(HALO, HALO)], buf.at[pl.ds(HALO + ROWS, HALO)], "rows", -1),
            (n + 1, buf.at[pl.ds(ROWS, HALO)], buf.at[pl.ds(0, HALO)], "rows", 1),
        ]

    hid_rows, g_rows = row_msgs(8, hb), row_msgs(10, gb)
    motion_cols = [
        (12, mb.at[own, last], edge_lo.at[2], "cols", 1),
        (13, mb.at[own, first], edge_hi.at[2], "cols", -1),
    ]
    motion_rows = row_msgs(14, mb)
    @pl.when(jnp.logical_not(has["cols", -1]))
    def _():
        edge_lo[...] = jnp.zeros_like(edge_lo)
        prev[...] = jnp.zeros_like(prev)
        tap_in[0] = jnp.zeros(tap_in.shape[1:], BF)
        part_in[...] = jnp.zeros_like(part_in)

    @pl.when(jnp.logical_not(has["cols", 1]))
    def _():
        edge_hi[...] = jnp.zeros_like(edge_hi)
        far_in[...] = jnp.zeros_like(far_in)
        left_in[...] = jnp.zeros_like(left_in)
        disp_next[...] = jnp.zeros_like(disp_next)
        tap_in[1] = jnp.zeros(tap_in.shape[1:], BF)

    @pl.when(jnp.logical_not(has["rows", -1]))
    def _():
        for buf in (hb, gb, mb):
            buf[0:HALO] = jnp.zeros((HALO, WIDE, CH), BF)

    @pl.when(jnp.logical_not(has["rows", 1]))
    def _():
        for buf in (hb, gb, mb):
            buf[HALO + ROWS : EXT] = jnp.zeros((HALO, WIDE, CH), BF)

    side = lax.broadcasted_iota(jnp.int32, (16, CH), 0) < 8

    def join_edges(which, buf):
        def one(r):
            hi = edge_hi[which, r].astype(F32)
            lo = edge_lo[which, r].astype(F32)
            buf[HALO + r, COLS:WIDE, :] = jnp.where(side, hi, lo).astype(BF)

        loop(0, ROWS, one, 8)

    sub = lax.broadcasted_iota(jnp.int32, (BAND, BAND), 0)
    lane = lax.broadcasted_iota(jnp.int32, (BAND, BAND), 1)
    ones = jnp.ones((BAND, BAND), BF)

    turn = (lax.broadcasted_iota(jnp.int32, (TAP_PAD, BAND), 0) == lax.broadcasted_iota(jnp.int32, (TAP_PAD, BAND), 1)).astype(BF)
    back = (sub == lane).astype(BF)[0:TAP_PAD]

    def spread_line(line):
        diag = jnp.where(sub == lane, line.astype(F32), 0.0).astype(BF)
        return mm(diag, ones).astype(jnp.int32)

    def spread(r, b):
        return spread_line(disp[r, :, b * BAND : (b + 1) * BAND])

    def usable_of(levels0):
        level = levels0 + lane - radius
        return (level >= 0) & (level < BAND) & (lane < taps)

    def clip(v):
        return jnp.clip(v, 0, BAND - 1)

    def finish_motion(r, b, pre):
        mpre[r, b * BAND : (b + 1) * BAND, :] = pre
        mb[HALO + r, b * BAND : (b + 1) * BAND, :] = (pre * sig(pre)).astype(BF)

    def near_row(n):
        for s in range(4):
            near_one(4 * n + s)

    def near_one(r):
        l0, l1 = fl[r, 0:BAND, :], fl[r, BAND:COLS, :]
        r0, r1 = fr[r, 0:BAND, :], fr[r, BAND:COLS, :]
        d0, d1 = spread(r, 0), spread(r, 1)
        c0 = sub + radius - d0 - lane
        tap_near[r] = jnp.where((c0 >= 0) & usable_of(d0), take(mm_nt(l0, r0) * scale, clip(c0)), 0.0)
        c1 = sub + radius - d1 - lane
        near = take(mm_nt(l1, r1) * scale, clip(c1))
        far = take(mm_nt(l1, r0) * scale, clip(c1 + BAND))
        tap = jnp.where(usable_of(d1), jnp.where(c1 >= 0, near, far), 0.0)
        finish_motion(r, 1, mm(tap.astype(BF), mwp[...]))

    for copy in copies[:2]:
        copy.wait()
    loop(0, ROWS // 4, near_row, 1)
    start(motion_cols[0])
    for copy in copies[2:4]:
        copy.wait()
    for spec in col_msgs:
        finish_recv(spec)
    join_edges(0, hb)
    join_edges(1, gb)
    for spec in hid_rows + g_rows:
        start(spec)

    for copy in copies[4:]:
        copy.wait()
    wcp[...] = jnp.zeros_like(wcp)
    wgp[...] = jnp.zeros_like(wgp)
    for a in range(3):
        for b in range(3):
            t = a * 3 + b
            blk = wc[t * 256 : (t + 1) * 256, :]
            wcp[a * 768 + b * 256 : a * 768 + (b + 1) * 256, 0:CH] = blk
            wcp[(a + 1) * 768 + b * 256 : (a + 1) * 768 + (b + 1) * 256, CH : 2 * CH] = blk
            wct[t * CH : (t + 1) * CH, :] = blk.astype(F32).T.astype(BF)
            turned = wg[t * 256 + CH : (t + 1) * 256, :].astype(F32).T.astype(BF)
            q = 2 - a
            wgp[q * 768 + b * 256 : q * 768 + (b + 1) * 256, 0:CH] = turned
            wgp[(q + 1) * 768 + b * 256 : (q + 1) * 768 + (b + 1) * 256, CH : 2 * CH] = turned


    for spec in hid_rows + g_rows:
        finish_recv(spec)

    def fill_hidden(r):
        put3(in3, r, 0, 256, hb[r].astype(F32), True)

    loop(0, EXT, fill_hidden, 4)

    def far_row(r):
        d0 = spread(r, 0)
        c0 = sub + radius - d0 - lane
        far = take(mm_nt(fl[r, 0:BAND, :], prev[r]) * scale, clip(c0 + BAND))
        tap = jnp.where((c0 < 0) & usable_of(d0), far, tap_near[r])
        finish_motion(r, 0, mm(tap.astype(BF), mwp[...]))

    def next_row(i):
        d = spread_line(disp_next[i, :, 0:BAND])
        c = sub + radius - d - lane
        far = take(mm_nt(left_in[i], fr[FWD + i, BAND:COLS, :]) * scale, clip(c + BAND))
        tap = jnp.where((c < 0) & usable_of(d), far, 0.0).astype(BF)
        tap_out[0, i] = mm_nt(turn, tap).astype(BF)

    def taken_row(i):
        pre = mm(tap_near[FWD + i].astype(BF), mwp[...])
        finish_motion(FWD + i, 0, pre + mm_tn(tap_in[0, i], mwp[0:TAP_PAD, :]))

    def over(chunk, body):
        loop(chunk[0], chunk[0] + chunk[1], body, chunk[1])

    finish_recv(disp_msg)
    for n, chunk in enumerate(BWD_CHUNKS):
        finish_recv(right_msgs[n])
        over(FWD_CHUNKS[n], far_row)
        finish_recv(left_msgs[n])
        over(chunk, next_row)
        start(tap_msgs[n])
    for n in range(len(BWD_CHUNKS), len(FWD_CHUNKS)):
        finish_recv(right_msgs[n])
        over(FWD_CHUNKS[n], far_row)
    for n, chunk in enumerate(BWD_CHUNKS):
        finish_recv(tap_msgs[n])
        over(chunk, taken_row)

    start(motion_cols[1])
    for spec in motion_cols:
        finish_recv(spec)
    join_edges(2, mb)
    for spec in motion_rows:
        start(spec)

    def fill_motion(r):
        m = mb[r].astype(F32)
        put3(in3, r, 1, 256, m, True)
        put3(ci3, r - 1, 1, 256, m, True)

    def rows_of(ref, r, count):
        return ref[pl.ds(r, count)].reshape(count * WIDE, ref.shape[2])

    def gate_pair(r):
        acc = mm(rows_of(in3, r - 1, 2), wg[0:768, :])
        acc = acc + mm(rows_of(in3, r, 2), wg[768:1536, :])
        acc = acc + mm(rows_of(in3, r + 1, 2), wg[1536:2304, :])
        for s in range(2):
            part = acc[s * WIDE : (s + 1) * WIDE]
            reset = sig(part[:, CH:])
            upd[r + s - 1] = sig(part[:, :CH])
            rst[r + s - 1] = reset
            put3(ci3, r + s - 1, 0, 256, reset * hb[r + s].astype(F32), True)

    loop(HALO, HALO + ROWS, fill_motion, 4)
    loop(0, ROWS // 2 - 1, lambda n: gate_pair(HALO + 1 + 2 * n), 2)
    for spec in motion_rows:
        finish_recv(spec)
    mb_top = EXT - 1
    loop(1, HALO, fill_motion, HALO - 1)
    loop(HALO + ROWS, mb_top, fill_motion, HALO - 1)
    put3(in3, 0, 1, 256, mb[0].astype(F32), True)
    put3(in3, mb_top, 1, 256, mb[mb_top].astype(F32), True)
    loop(0, 2, lambda n: gate_pair(1 + 2 * n), 2)
    loop(0, 2, lambda n: gate_pair(HALO + ROWS - 1 + 2 * n), 2)

    def cand_quad(n, kept):
        r = 2 + 4 * n
        acc = None
        for q in range(4):
            lhs = jnp.concatenate([ci3[r - 2 + q], ci3[r + q]], axis=0)
            term = mm(lhs, wcp[q * 768 : (q + 1) * 768, :])
            acc = term if acc is None else acc + term
        for s in range(4):
            c = jnp.tanh(acc[(s // 2) * WIDE : (s // 2 + 1) * WIDE, (s % 2) * CH : (s % 2 + 1) * CH])
            u = upd[r + s - 1]
            h = hb[r + s].astype(F32)
            g = gb[r + s].astype(F32)
            if kept[s]:
                nh[r + s - HALO] = ((1.0 - u) * h + u * c)[:COLS].astype(BF)
            put3(cg3, r + s - 2, 0, CH, g * u * (1.0 - c * c), False)
            put3(in3, r + s, 0, 256, g * (c - h) * u * (1.0 - u), False)

    cand_quad(0, (False, False, True, True))
    loop(1, 4, lambda n: cand_quad(n, (True,) * 4), 1)
    cand_quad(4, (True, True, False, False))

    def back_pair(n):
        r = HALO - 1 + 2 * n
        acc = mm(rows_of(cg3, r - 1, 2), wct[0:384, :])
        acc = acc + mm(rows_of(cg3, r - 2, 2), wct[384:768, :])
        acc = acc + mm(rows_of(cg3, r - 3, 2), wct[768:1152, :])
        for s in range(2):
            part = acc[s * WIDE : (s + 1) * WIDE]
            reset = rst[r + s - 1]
            grad = part[:, :CH] * hb[r + s].astype(F32) * reset * (1.0 - reset)
            put3(in3, r + s, 1, 256, grad, False)
            cbm[r + s - 3] = part[:, CH:]

    loop(0, ROWS // 2 + 1, back_pair, 3)

    def slopes(n, b, store):
        r = HALO + 4 * n
        cut = slice(b * BAND, (b + 1) * BAND)
        acc = None
        for q in range(4):
            lhs = jnp.concatenate([in3[r - 1 + q, cut], in3[r + 1 + q, cut]], axis=0)
            term = mm(lhs, wgp[q * 768 : (q + 1) * 768, :])
            acc = term if acc is None else acc + term
        for s in range(4):
            row = 4 * n + s
            half = acc[(s // 2) * BAND : (s // 2 + 1) * BAND, (s % 2) * CH : (s % 2 + 1) * CH]
            motion_grad = half + cbm[row + 1, cut]
            pre = mpre[row, cut]
            sg = sig(pre)
            pre_grad = (motion_grad * sg * (1.0 + pre * (1.0 - sg))).astype(BF)
            d = spread(row, b)
            tap = jnp.where(usable_of(d), mm_nt(pre_grad, mwp[...]), 0.0)
            store(row, d, tap)

    def g_of(tap, d, shift):
        k = sub + (radius + shift) - d - lane
        return jnp.where(k >= 0, take(tap, clip(k)), 0.0).astype(BF)

    def keep_tap(row, d, tap):
        tap_near[row] = tap
        if row >= FWD:
            tap_out[1, row - FWD] = mm_nt(turn, tap.astype(BF)).astype(BF)

    def send_far(r):
        g_far = g_of(tap_near[r], spread(r, 0), BAND)
        far_out[r] = (mm_tn(g_far, fl[r, 0:BAND, :]) * scale).astype(BF)

    def send_part(i):
        d = spread_line(disp_next[i, :, 0:BAND])
        tap = mm_tn(tap_in[1, i], back)
        g_far = g_of(tap, d, BAND)
        part_out[i] = (mm(g_far, fr[FWD + i, BAND:COLS, :]) * scale).astype(BF)
        near1[FWD + i] = mm_tn(g_far, left_in[i]) * scale

    def own_second(row, d, tap):
        g_near, g_far = g_of(tap, d, 0), g_of(tap, d, BAND)
        l0, l1 = fl[row, 0:BAND, :], fl[row, BAND:COLS, :]
        r0, r1 = fr[row, 0:BAND, :], fr[row, BAND:COLS, :]
        gl[row, BAND:COLS, :] = ((mm(g_near, r1) + mm(g_far, r0)) * scale).astype(BF)
        g_first = g_of(tap_near[row], spread(row, 0), 0)
        far = (mm_tn(g_far, l1) * scale).astype(BF).astype(F32)
        gr[row, 0:BAND, :] = (mm_tn(g_first, l0) * scale + far).astype(BF)
        near = mm_tn(g_near, l1) * scale
        first = mm(g_first, r0)

        if row < FWD:
            g_back = g_of(tap_near[row], spread(row, 0), BAND)
            gl[row, 0:BAND, :] = ((first + mm(g_back, prev[row])) * scale).astype(BF)
            near1[row] = near
        else:
            gr[row, BAND:COLS, :] = (near + near1[row].astype(BF).astype(F32)).astype(BF)
            near1[row] = first * scale

    quads = ROWS // 4
    split = FWD // 4
    for n in range(split, quads):
        slopes(n, 0, keep_tap)
    for spec in slope_msgs:
        start(spec)
    for n in range(split):
        slopes(n, 0, keep_tap)
    for n, chunk in enumerate(FWD_CHUNKS):
        over(chunk, send_far)
        start(far_msgs[n])
    for n, chunk in enumerate(BWD_CHUNKS):
        finish_recv(slope_msgs[n])
        over(chunk, send_part)
        start(part_msgs[n])
    for n in range(quads):
        slopes(n, 1, own_second)

    def add_far(r):
        gr[r, BAND:COLS, :] = (near1[r] + far_in[r].astype(F32)).astype(BF)

    def add_part(i):
        gl[FWD + i, 0:BAND, :] = (near1[FWD + i] + part_in[i].astype(F32)).astype(BF)

    for n, chunk in enumerate(FWD_CHUNKS):
        finish_recv(far_msgs[n])
        over(chunk, add_far)
    for n, chunk in enumerate(BWD_CHUNKS):
        finish_recv(part_msgs[n])
        over(chunk, add_part)
    sent = col_msgs + [disp_msg] + left_msgs + right_msgs + hid_rows + g_rows + motion_cols + motion_rows
    for spec in sent + tap_msgs + slope_msgs + far_msgs + part_msgs:
        finish_send(spec)


def per_device(n_rows, n_cols, feat_left, feat_right, hidden, disparity, motion_weight, gate_weight, cand_weight, grad_hidden):
    taps = motion_weight.shape[0]
    feat = feat_left.shape[2]
    wg = gate_weight.reshape(9 * 256, 256)
    wc = cand_weight.reshape(9 * 256, CH)
    hbm = pl.BlockSpec(memory_space=pl.ANY)
    vmem = pl.BlockSpec(memory_space=pltpu.VMEM)
    v = pltpu.VMEM
    return pl.pallas_call(
        functools.partial(kernel, n_rows, n_cols, taps, 1.0 / math.sqrt(feat)),
        out_shape=(
            jax.ShapeDtypeStruct(hidden.shape, BF),
            jax.ShapeDtypeStruct(feat_left.shape, BF),
            jax.ShapeDtypeStruct(feat_right.shape, BF),
        ),
        in_specs=[hbm] * 6 + [vmem] * 2,
        out_specs=(vmem,) * 3,
        scratch_shapes=[
            v((ROWS, COLS, feat), BF),
            v((ROWS, COLS, feat), BF),
            v((FWD, BAND, feat), BF),
            v((BWD, BAND, feat), BF),
            v((BWD, 1, COLS), jnp.int32),
            v((FWD, BAND, feat), BF),
            v((FWD, BAND, feat), BF),
            v((BWD, BAND, feat), BF),
            v((BWD, BAND, feat), BF),
            v((2, BWD, TAP_PAD, BAND), BF),
            v((2, BWD, TAP_PAD, BAND), BF),
            v((ROWS, BAND, feat), F32),
            v((ROWS, BAND, BAND), F32),
            v((ROWS, 1, COLS), jnp.int32),
            v((BAND, CH), BF),
            v((EXT, WIDE, CH), BF),
            v((EXT, WIDE, CH), BF),
            v((EXT, WIDE, CH), BF),
            v((EXT, WIDE, 6 * CH), BF),
            v((EXT - 2, WIDE, 6 * CH), BF),
            v((EXT - 4, WIDE, 3 * CH), BF),
            v((EXT - 2, WIDE, CH), F32),
            v((EXT - 2, WIDE, CH), F32),
            v((ROWS, COLS, CH), F32),
            v((ROWS + 2, WIDE, CH), F32),
            v((9 * 256, 256), BF),
            v((9 * 256, CH), BF),
            v((12 * 256, 256), BF),
            v((9 * CH, 256), BF),
            v((12 * 256, 256), BF),
            v((3, ROWS, 16, CH), BF),
            v((3, ROWS, 16, CH), BF),
            pltpu.SemaphoreType.DMA((6,)),
            pltpu.SemaphoreType.DMA((N_MSG,)),
            pltpu.SemaphoreType.DMA((N_MSG,)),
        ],
        compiler_params=pltpu.CompilerParams(
            collective_id=0, has_side_effects=True, vmem_limit_bytes=63 * 1024 * 1024
        ),
        cost_estimate=pl.CostEstimate(flops=17 * 10**9, bytes_accessed=14 * 10**6, transcendentals=0),
    )(feat_left, feat_right, hidden, grad_hidden, wg, wc, disparity, motion_weight)


def solution(mesh):
    blocks = P("rows", "cols", None)
    return jax.shard_map(
        functools.partial(per_device, mesh.shape["rows"], mesh.shape["cols"]),
        mesh=mesh,
        in_specs=(blocks, blocks, blocks, P("rows", "cols"), P(), P(), P(), blocks),
        out_specs=(blocks, blocks, blocks),
        check_vma=False,
    )
```

```python
import functools
import math

import jax
import jax.numpy as jnp
from jax import lax
from jax.experimental import pallas as pl
from jax.experimental.pallas import tpu as pltpu
from jax.sharding import PartitionSpec as P

MESH = pl.DeviceIdType.MESH
F32 = jnp.float32
BF = jnp.bfloat16
BAND = 128
ROWS = 16
COLS = 256
WIDE = COLS + 16
HALO = 4
EXT = ROWS + 2 * HALO
CH = 128
FWD = 9
BWD = ROWS - FWD
TAP_PAD = 16
FWD_CHUNKS = ((0, 3), (3, 3), (6, 3))
BWD_CHUNKS = ((0, 4), (4, 3))
N_MSG = 17 + 2 * len(FWD_CHUNKS) + 4 * len(BWD_CHUNKS)


def mm(a, b):
    return jnp.dot(a, b, preferred_element_type=F32)


def mm_nt(a, b):
    return lax.dot_general(a, b, (((1,), (1,)), ((), ())), preferred_element_type=F32)


def mm_tn(a, b):
    return lax.dot_general(a, b, (((0,), (0,)), ((), ())), preferred_element_type=F32)


def sig(v):
    return 0.5 * jnp.tanh(0.5 * v) + 0.5


def put3(places, part, stride, val, forward):
    low = pltpu.roll(val, 1, 0)
    high = pltpu.roll(val, WIDE - 1, 0)
    order = (low, val, high) if forward else (high, val, low)
    for b in range(3):
        at = b * stride + part * CH
        kept = order[b].astype(BF)
        for ref, row in places:
            ref[row, :, at : at + CH] = kept


def loop(low, high, body, by):
    whole = (high - low) // by

    def step(n, carry):
        for s in range(by):
            body(low + n * by + s)
        return carry

    if whole > 1:
        lax.fori_loop(0, whole, step, 0)
    elif whole == 1:
        step(0, 0)
    for n in range(low + whole * by, high):
        body(n)


def take(values, index):
    return jnp.take_along_axis(values, index, axis=1, mode="promise_in_bounds")


def kernel(
    n_rows, n_cols, taps, scale,
    fl_hbm, fr_hbm, hid_hbm, g_hbm, wg_hbm, wc_hbm, disp_in, mw,
    nh, gl, gr,
    fl, fr, prev, left_in, disp_next, far_out, far_in, part_out, part_in, tap_out, tap_in,
    near1, tap_near, cols, disp, mwp,
    hb, gb, mb, in3, ci3, cg3, upd, rst, mpre, cbm,
    wg, wc, wcp, wct, wgp, edge_lo, edge_hi,
    local, send, recv,
):
    rid = lax.axis_index("rows")
    cid = lax.axis_index("cols")
    radius = taps // 2

    has = {
        ("rows", -1): rid > 0,
        ("rows", 1): rid < n_rows - 1,
        ("cols", -1): cid > 0,
        ("cols", 1): cid < n_cols - 1,
    }

    def target(axis, step):
        return (rid + step, cid) if axis == "rows" else (rid, cid + step)

    def message(n, src, dst, axis, step):
        return pltpu.make_async_remote_copy(
            src_ref=src, dst_ref=dst, send_sem=send.at[n], recv_sem=recv.at[n],
            device_id=target(axis, step), device_id_type=MESH,
        )

    def start(spec):
        @pl.when(has[spec[3], spec[4]])
        def _():
            message(*spec).start()

    def finish_send(spec):
        @pl.when(has[spec[3], spec[4]])
        def _():
            message(*spec).wait_send()

    def finish_recv(spec):
        @pl.when(has[spec[3], -spec[4]])
        def _():
            message(*spec).wait_recv()

    own = pl.ds(HALO, ROWS)
    main = pl.ds(0, COLS)
    copies = [
        pltpu.make_async_copy(src, dst, local.at[n])
        for n, (src, dst) in enumerate(
            [
                (fl_hbm, fl),
                (fr_hbm, fr),
                (hid_hbm, hb.at[own, main]),
                (g_hbm, gb.at[own, main]),
                (wg_hbm, wg),
                (wc_hbm, wc),
            ]
        )
    ]
    for copy in copies:
        copy.start()

    barrier = pltpu.get_barrier_semaphore()
    for (axis, step), there in has.items():
        @pl.when(there)
        def _(axis=axis, step=step):
            pl.semaphore_signal(barrier, inc=1, device_id=target(axis, step), device_id_type=MESH)
    peers = sum(there.astype(jnp.int32) for there in has.values())
    pl.semaphore_wait(barrier, peers)

    last = pl.ds(COLS - 16, 16)
    first = pl.ds(0, 16)
    col_msgs = [
        (0, hid_hbm.at[:, last], edge_lo.at[0], "cols", 1),
        (1, hid_hbm.at[:, first], edge_hi.at[0], "cols", -1),
        (2, g_hbm.at[:, last], edge_lo.at[1], "cols", 1),
        (3, g_hbm.at[:, first], edge_hi.at[1], "cols", -1),
    ]
    bands = pl.ds(0, BAND)
    tail_band = pl.ds(COLS - BAND, BAND)
    base = 17
    right_msgs, left_msgs, tap_msgs, slope_msgs, far_msgs, part_msgs = [], [], [], [], [], []
    for at, size in FWD_CHUNKS:
        rows = pl.ds(at, size)
        right_msgs.append((base, fr_hbm.at[rows, tail_band], prev.at[rows], "cols", 1))
        far_msgs.append((base + 1, far_out.at[rows], far_in.at[rows], "cols", -1))
        base += 2
    for at, size in BWD_CHUNKS:
        rows, whole = pl.ds(at, size), pl.ds(FWD + at, size)
        left_msgs.append((base, fl_hbm.at[whole, bands], left_in.at[rows], "cols", -1))
        tap_msgs.append((base + 1, tap_out.at[0, rows], tap_in.at[0, rows], "cols", 1))
        slope_msgs.append((base + 2, tap_out.at[1, rows], tap_in.at[1, rows], "cols", -1))
        part_msgs.append((base + 3, part_out.at[rows], part_in.at[rows], "cols", 1))
        base += 4
    disp_msg = (16, disp.at[pl.ds(FWD, BWD)], disp_next, "cols", -1)
    for r in range(ROWS):
        disp[r] = disp_in[r : r + 1, :]
    for spec in col_msgs + [disp_msg] + left_msgs + right_msgs:
        start(spec)
    mwp[...] = jnp.zeros_like(mwp)
    mwp[0:taps, :] = mw[...]

    def row_msgs(n, buf):
        return [
            (n, buf.at[pl.ds(HALO, HALO)], buf.at[pl.ds(HALO + ROWS, HALO)], "rows", -1),
            (n + 1, buf.at[pl.ds(ROWS, HALO)], buf.at[pl.ds(0, HALO)], "rows", 1),
        ]

    hid_rows, g_rows = row_msgs(8, hb), row_msgs(10, gb)
    motion_cols = [
        (12, mb.at[own, last], edge_lo.at[2], "cols", 1),
        (13, mb.at[own, first], edge_hi.at[2], "cols", -1),
    ]
    motion_rows = row_msgs(14, mb)
    @pl.when(jnp.logical_not(has["cols", -1]))
    def _():
        edge_lo[...] = jnp.zeros_like(edge_lo)
        prev[...] = jnp.zeros_like(prev)
        tap_in[0] = jnp.zeros(tap_in.shape[1:], BF)
        part_in[...] = jnp.zeros_like(part_in)

    @pl.when(jnp.logical_not(has["cols", 1]))
    def _():
        edge_hi[...] = jnp.zeros_like(edge_hi)
        far_in[...] = jnp.zeros_like(far_in)
        left_in[...] = jnp.zeros_like(left_in)
        disp_next[...] = jnp.zeros_like(disp_next)
        tap_in[1] = jnp.zeros(tap_in.shape[1:], BF)

    @pl.when(jnp.logical_not(has["rows", -1]))
    def _():
        for buf in (hb, gb, mb):
            buf[0:HALO] = jnp.zeros((HALO, WIDE, CH), BF)

    @pl.when(jnp.logical_not(has["rows", 1]))
    def _():
        for buf in (hb, gb, mb):
            buf[HALO + ROWS : EXT] = jnp.zeros((HALO, WIDE, CH), BF)

    side = lax.broadcasted_iota(jnp.int32, (16, CH), 0) < 8

    def join_edges(which, buf):
        def one(r):
            hi = edge_hi[which, r].astype(F32)
            lo = edge_lo[which, r].astype(F32)
            buf[HALO + r, COLS:WIDE, :] = jnp.where(side, hi, lo).astype(BF)

        loop(0, ROWS, one, 8)

    sub = lax.broadcasted_iota(jnp.int32, (BAND, BAND), 0)
    lane = lax.broadcasted_iota(jnp.int32, (BAND, BAND), 1)
    ones = jnp.ones((BAND, BAND), BF)

    turn = (lax.broadcasted_iota(jnp.int32, (TAP_PAD, BAND), 0) == lax.broadcasted_iota(jnp.int32, (TAP_PAD, BAND), 1)).astype(BF)
    back = (sub == lane).astype(BF)[0:TAP_PAD]

    def spread_line(line):
        diag = jnp.where(sub == lane, line.astype(F32), 0.0).astype(BF)
        return mm(diag, ones).astype(jnp.int32)

    def column_of(line):
        return sub + radius - spread_line(line) - lane

    def usable_of(col):
        level = sub - col
        return (level >= 0) & (level < BAND) & (lane < taps)

    def pick(values, col):
        return take(values, col & (BAND - 1))

    def g_of(picked, col, shift):
        return jnp.where(((col + shift) & -TAP_PAD) == 0, picked, 0.0).astype(BF)

    def finish_motion(r, b, pre):
        mpre[r, b * BAND : (b + 1) * BAND, :] = pre
        mb[HALO + r, b * BAND : (b + 1) * BAND, :] = (pre * sig(pre)).astype(BF)

    def near_row(n):
        for s in range(4):
            near_one(4 * n + s)

    def near_one(r):
        c0 = column_of(disp[r, :, 0:BAND])
        c1 = column_of(disp[r, :, BAND:COLS])
        cols[0, r] = c0
        cols[1, r] = c1
        near = pick(mm_nt(fl[r, 0:BAND, :], fr[r, 0:BAND, :]), c0)
        tap_near[r] = jnp.where((c0 >= 0) & usable_of(c0), near, 0.0) * scale
        both = mm_nt(fl[r, BAND:COLS, :], fr[r])
        tap = jnp.where(c1 >= 0, pick(both[:, BAND:], c1), pick(both[:, :BAND], c1))
        tap = jnp.where(usable_of(c1), tap, 0.0) * scale
        finish_motion(r, 1, mm(tap.astype(BF), mwp[...]))

    for copy in copies[:2]:
        copy.wait()
    loop(0, ROWS // 4, near_row, 1)
    start(motion_cols[0])
    for copy in copies[2:4]:
        copy.wait()
    for spec in col_msgs:
        finish_recv(spec)
    join_edges(0, hb)
    join_edges(1, gb)
    for spec in hid_rows + g_rows:
        start(spec)

    for copy in copies[4:]:
        copy.wait()
    wcp[...] = jnp.zeros_like(wcp)
    wgp[...] = jnp.zeros_like(wgp)
    for a in range(3):
        for b in range(3):
            t = a * 3 + b
            blk = wc[t * 256 : (t + 1) * 256, :]
            wcp[a * 768 + b * 256 : a * 768 + (b + 1) * 256, 0:CH] = blk
            wcp[(a + 1) * 768 + b * 256 : (a + 1) * 768 + (b + 1) * 256, CH : 2 * CH] = blk
            wct[t * CH : (t + 1) * CH, :] = blk.astype(F32).T.astype(BF)
            turned = wg[t * 256 + CH : (t + 1) * 256, :].astype(F32).T.astype(BF)
            q = 2 - a
            wgp[q * 768 + b * 256 : q * 768 + (b + 1) * 256, 0:CH] = turned
            wgp[(q + 1) * 768 + b * 256 : (q + 1) * 768 + (b + 1) * 256, CH : 2 * CH] = turned


    for spec in hid_rows + g_rows:
        finish_recv(spec)

    def fill_hidden(r):
        put3(((in3, r),), 0, 256, hb[r].astype(F32), True)

    loop(0, EXT, fill_hidden, 4)

    def far_row(r):
        c0 = cols[0, r]
        far = pick(mm_nt(fl[r, 0:BAND, :], prev[r]), c0) * scale
        tap = jnp.where((c0 < 0) & usable_of(c0), far, tap_near[r])
        finish_motion(r, 0, mm(tap.astype(BF), mwp[...]))

    def next_row(i):
        c = column_of(disp_next[i, :, 0:BAND])
        far = pick(mm_nt(left_in[i], fr[FWD + i, BAND:COLS, :]), c) * scale
        tap = jnp.where((c < 0) & usable_of(c), far, 0.0).astype(BF)
        tap_out[0, i] = mm_nt(turn, tap).astype(BF)

    def taken_row(i):
        pre = mm(tap_near[FWD + i].astype(BF), mwp[...])
        finish_motion(FWD + i, 0, pre + mm_tn(tap_in[0, i], mwp[0:TAP_PAD, :]))

    def over(chunk, body):
        loop(chunk[0], chunk[0] + chunk[1], body, chunk[1])

    finish_recv(disp_msg)
    for n, chunk in enumerate(BWD_CHUNKS):
        finish_recv(right_msgs[n])
        over(FWD_CHUNKS[n], far_row)
        finish_recv(left_msgs[n])
        over(chunk, next_row)
        start(tap_msgs[n])
    for n in range(len(BWD_CHUNKS), len(FWD_CHUNKS)):
        finish_recv(right_msgs[n])
        over(FWD_CHUNKS[n], far_row)
    for n, chunk in enumerate(BWD_CHUNKS):
        finish_recv(tap_msgs[n])
        over(chunk, taken_row)

    start(motion_cols[1])
    for spec in motion_cols:
        finish_recv(spec)
    join_edges(2, mb)
    for spec in motion_rows:
        start(spec)

    def fill_motion(r):
        m = mb[r].astype(F32)
        put3(((in3, r), (ci3, r - 1)), 1, 256, m, True)

    def rows_of(ref, r, count):
        return ref[pl.ds(r, count)].reshape(count * WIDE, ref.shape[2])

    def gate_pair(r):
        acc = mm(rows_of(in3, r - 1, 2), wg[0:768, :])
        acc = acc + mm(rows_of(in3, r, 2), wg[768:1536, :])
        acc = acc + mm(rows_of(in3, r + 1, 2), wg[1536:2304, :])
        for s in range(2):
            part = acc[s * WIDE : (s + 1) * WIDE]
            reset = sig(part[:, CH:])
            upd[r + s - 1] = sig(part[:, :CH])
            rst[r + s - 1] = reset
            put3(((ci3, r + s - 1),), 0, 256, reset * hb[r + s].astype(F32), True)

    loop(HALO, HALO + ROWS, fill_motion, 4)
    loop(0, ROWS // 2 - 1, lambda n: gate_pair(HALO + 1 + 2 * n), 2)
    for spec in motion_rows:
        finish_recv(spec)
    mb_top = EXT - 1
    loop(1, HALO, fill_motion, HALO - 1)
    loop(HALO + ROWS, mb_top, fill_motion, HALO - 1)
    put3(((in3, 0),), 1, 256, mb[0].astype(F32), True)
    put3(((in3, mb_top),), 1, 256, mb[mb_top].astype(F32), True)
    loop(0, 2, lambda n: gate_pair(1 + 2 * n), 2)
    loop(0, 2, lambda n: gate_pair(HALO + ROWS - 1 + 2 * n), 2)

    def cand_quad(n, kept):
        r = 2 + 4 * n
        acc = None
        for q in range(4):
            lhs = jnp.concatenate([ci3[r - 2 + q], ci3[r + q]], axis=0)
            term = mm(lhs, wcp[q * 768 : (q + 1) * 768, :])
            acc = term if acc is None else acc + term
        for s in range(4):
            c = jnp.tanh(acc[(s // 2) * WIDE : (s // 2 + 1) * WIDE, (s % 2) * CH : (s % 2 + 1) * CH])
            u = upd[r + s - 1]
            h = hb[r + s].astype(F32)
            g = gb[r + s].astype(F32)
            if kept[s]:
                nh[r + s - HALO] = ((1.0 - u) * h + u * c)[:COLS].astype(BF)
            put3(((cg3, r + s - 2),), 0, CH, g * u * (1.0 - c * c), False)
            put3(((in3, r + s),), 0, 256, g * (c - h) * u * (1.0 - u), False)

    cand_quad(0, (False, False, True, True))
    loop(1, 4, lambda n: cand_quad(n, (True,) * 4), 1)
    cand_quad(4, (True, True, False, False))

    def back_pair(n):
        r = HALO - 1 + 2 * n
        acc = mm(rows_of(cg3, r - 1, 2), wct[0:384, :])
        acc = acc + mm(rows_of(cg3, r - 2, 2), wct[384:768, :])
        acc = acc + mm(rows_of(cg3, r - 3, 2), wct[768:1152, :])
        for s in range(2):
            part = acc[s * WIDE : (s + 1) * WIDE]
            reset = rst[r + s - 1]
            grad = part[:, :CH] * hb[r + s].astype(F32) * reset * (1.0 - reset)
            put3(((in3, r + s),), 1, 256, grad, False)
            cbm[r + s - 3] = part[:, CH:]

    loop(0, ROWS // 2 + 1, back_pair, 3)

    def slopes(n, b, store):
        r = HALO + 4 * n
        cut = slice(b * BAND, (b + 1) * BAND)
        acc = None
        for q in range(4):
            lhs = jnp.concatenate([in3[r - 1 + q, cut], in3[r + 1 + q, cut]], axis=0)
            term = mm(lhs, wgp[q * 768 : (q + 1) * 768, :])
            acc = term if acc is None else acc + term
        for s in range(4):
            row = 4 * n + s
            half = acc[(s // 2) * BAND : (s // 2 + 1) * BAND, (s % 2) * CH : (s % 2 + 1) * CH]
            motion_grad = half + cbm[row + 1, cut]
            pre = mpre[row, cut]
            sg = sig(pre)
            pre_grad = (motion_grad * sg * (1.0 + pre * (1.0 - sg))).astype(BF)
            col = cols[b, row]
            tap = jnp.where(usable_of(col), mm_nt(pre_grad, mwp[...]), 0.0)
            store(row, col, tap)

    def keep_tap(row, col, tap):
        tap_near[row] = pick(tap, col)
        if row >= FWD:
            tap_out[1, row - FWD] = mm_nt(turn, tap.astype(BF)).astype(BF)

    def send_far(r):
        g_far = g_of(tap_near[r], cols[0, r], BAND)
        far_out[r] = (mm_tn(g_far, fl[r, 0:BAND, :]) * scale).astype(BF)

    def send_part(i):
        col = column_of(disp_next[i, :, 0:BAND])
        g_far = g_of(pick(mm_tn(tap_in[1, i], back), col), col, BAND)
        part_out[i] = (mm(g_far, fr[FWD + i, BAND:COLS, :]) * scale).astype(BF)
        near1[FWD + i] = mm_tn(g_far, left_in[i]) * scale

    def own_second(row, col, tap):
        picked = pick(tap, col)
        g_both = jnp.concatenate([g_of(picked, col, BAND), g_of(picked, col, 0)], axis=1)
        gl[row, BAND:COLS, :] = (mm(g_both, fr[row]) * scale).astype(BF)
        grads = mm_tn(g_both, fl[row, BAND:COLS, :]) * scale
        col0 = cols[0, row]
        g_first = g_of(tap_near[row], col0, 0)
        far = grads[:BAND].astype(BF).astype(F32)
        gr[row, 0:BAND, :] = (mm_tn(g_first, fl[row, 0:BAND, :]) * scale + far).astype(BF)
        near = grads[BAND:]
        first = mm(g_first, fr[row, 0:BAND, :])

        if row < FWD:
            g_back = g_of(tap_near[row], col0, BAND)
            gl[row, 0:BAND, :] = ((first + mm(g_back, prev[row])) * scale).astype(BF)
            near1[row] = near
        else:
            gr[row, BAND:COLS, :] = (near + near1[row].astype(BF).astype(F32)).astype(BF)
            near1[row] = first * scale

    quads = ROWS // 4
    split = FWD // 4
    for n in range(split, quads):
        slopes(n, 0, keep_tap)
    for spec in slope_msgs:
        start(spec)
    for n in range(split):
        slopes(n, 0, keep_tap)
    for n, chunk in enumerate(FWD_CHUNKS):
        over(chunk, send_far)
        start(far_msgs[n])
    for n, chunk in enumerate(BWD_CHUNKS):
        finish_recv(slope_msgs[n])
        over(chunk, send_part)
        start(part_msgs[n])
    for n in range(quads):
        slopes(n, 1, own_second)

    def add_far(r):
        gr[r, BAND:COLS, :] = (near1[r] + far_in[r].astype(F32)).astype(BF)

    def add_part(i):
        gl[FWD + i, 0:BAND, :] = (near1[FWD + i] + part_in[i].astype(F32)).astype(BF)

    for n, chunk in enumerate(FWD_CHUNKS):
        finish_recv(far_msgs[n])
        over(chunk, add_far)
    for n, chunk in enumerate(BWD_CHUNKS):
        finish_recv(part_msgs[n])
        over(chunk, add_part)
    sent = col_msgs + [disp_msg] + left_msgs + right_msgs + hid_rows + g_rows + motion_cols + motion_rows
    for spec in sent + tap_msgs + slope_msgs + far_msgs + part_msgs:
        finish_send(spec)


def hand_on(*refs):
    half = len(refs) // 2
    for src, dst in zip(refs[:half], refs[half:]):
        dst[...] = src[...]


def whole_copy(*arrays):
    specs = [pl.BlockSpec((4,) + a.shape[1:], lambda i: (i, 0, 0)) for a in arrays]
    return pl.pallas_call(
        hand_on,
        grid=(ROWS // 4,),
        out_shape=tuple(jax.ShapeDtypeStruct(a.shape, a.dtype) for a in arrays),
        in_specs=specs,
        out_specs=tuple(specs),
    )(*arrays)


def per_device(n_rows, n_cols, feat_left, feat_right, hidden, disparity, motion_weight, gate_weight, cand_weight, grad_hidden):
    taps = motion_weight.shape[0]
    feat = feat_left.shape[2]
    wg = gate_weight.reshape(9 * 256, 256)
    wc = cand_weight.reshape(9 * 256, CH)
    hbm = pl.BlockSpec(memory_space=pl.ANY)
    vmem = pl.BlockSpec(memory_space=pltpu.VMEM)
    v = pltpu.VMEM
    outs = pl.pallas_call(
        functools.partial(kernel, n_rows, n_cols, taps, 1.0 / math.sqrt(feat)),
        out_shape=(
            jax.ShapeDtypeStruct(hidden.shape, BF),
            jax.ShapeDtypeStruct(feat_left.shape, BF),
            jax.ShapeDtypeStruct(feat_right.shape, BF),
        ),
        in_specs=[hbm] * 6 + [vmem] * 2,
        out_specs=(vmem,) * 3,
        scratch_shapes=[
            v((ROWS, COLS, feat), BF),
            v((ROWS, COLS, feat), BF),
            v((FWD, BAND, feat), BF),
            v((BWD, BAND, feat), BF),
            v((BWD, 1, COLS), jnp.int32),
            v((FWD, BAND, feat), BF),
            v((FWD, BAND, feat), BF),
            v((BWD, BAND, feat), BF),
            v((BWD, BAND, feat), BF),
            v((2, BWD, TAP_PAD, BAND), BF),
            v((2, BWD, TAP_PAD, BAND), BF),
            v((ROWS, BAND, feat), F32),
            v((ROWS, BAND, BAND), F32),
            v((2, ROWS, BAND, BAND), jnp.int32),
            v((ROWS, 1, COLS), jnp.int32),
            v((BAND, CH), BF),
            v((EXT, WIDE, CH), BF),
            v((EXT, WIDE, CH), BF),
            v((EXT, WIDE, CH), BF),
            v((EXT, WIDE, 6 * CH), BF),
            v((EXT - 2, WIDE, 6 * CH), BF),
            v((EXT - 4, WIDE, 3 * CH), BF),
            v((EXT - 2, WIDE, CH), F32),
            v((EXT - 2, WIDE, CH), F32),
            v((ROWS, COLS, CH), F32),
            v((ROWS + 2, WIDE, CH), F32),
            v((9 * 256, 256), BF),
            v((9 * 256, CH), BF),
            v((12 * 256, 256), BF),
            v((9 * CH, 256), BF),
            v((12 * 256, 256), BF),
            v((3, ROWS, 16, CH), BF),
            v((3, ROWS, 16, CH), BF),
            pltpu.SemaphoreType.DMA((6,)),
            pltpu.SemaphoreType.DMA((N_MSG,)),
            pltpu.SemaphoreType.DMA((N_MSG,)),
        ],
        compiler_params=pltpu.CompilerParams(
            collective_id=0, has_side_effects=True, vmem_limit_bytes=63 * 1024 * 1024
        ),
        cost_estimate=pl.CostEstimate(flops=17 * 10**9, bytes_accessed=14 * 10**6, transcendentals=0),
    )(feat_left, feat_right, hidden, grad_hidden, wg, wc, disparity, motion_weight)
    return whole_copy(*outs)


def solution(mesh):
    blocks = P("rows", "cols", None)
    return jax.shard_map(
        functools.partial(per_device, mesh.shape["rows"], mesh.shape["cols"]),
        mesh=mesh,
        in_specs=(blocks, blocks, blocks, P("rows", "cols"), P(), P(), P(), blocks),
        out_specs=(blocks, blocks, blocks),
        check_vma=False,
    )
```

```python
import functools
import math

import jax
import jax.numpy as jnp
from jax import lax
from jax.experimental import pallas as pl
from jax.experimental.pallas import tpu as pltpu
from jax.sharding import PartitionSpec as P

MESH = pl.DeviceIdType.MESH
F32 = jnp.float32
BF = jnp.bfloat16
BAND = 128
ROWS = 16
COLS = 256
WIDE = COLS + 16
HALO = 4
EXT = ROWS + 2 * HALO
CH = 128
FWD = 9
BWD = ROWS - FWD
TAP_PAD = 16
FWD_CHUNKS = ((0, 3), (3, 3), (6, 3))
BWD_CHUNKS = ((0, 4), (4, 3))
N_MSG = 17 + 2 * len(FWD_CHUNKS) + 4 * len(BWD_CHUNKS)


def mm(a, b):
    return jnp.dot(a, b, preferred_element_type=F32)


def mm_nt(a, b):
    return lax.dot_general(a, b, (((1,), (1,)), ((), ())), preferred_element_type=F32)


def mm_tn(a, b):
    return lax.dot_general(a, b, (((0,), (0,)), ((), ())), preferred_element_type=F32)


def sig(v):
    return 0.5 * jnp.tanh(0.5 * v) + 0.5


def put3(places, part, stride, val, forward):
    low = pltpu.roll(val, 1, 0)
    high = pltpu.roll(val, WIDE - 1, 0)
    order = (low, val, high) if forward else (high, val, low)
    for b in range(3):
        at = b * stride + part * CH
        kept = order[b].astype(BF)
        for ref, row in places:
            ref[row, :, at : at + CH] = kept


def loop(low, high, body, by):
    whole = (high - low) // by

    def step(n, carry):
        for s in range(by):
            body(low + n * by + s)
        return carry

    if whole > 1:
        lax.fori_loop(0, whole, step, 0)
    elif whole == 1:
        step(0, 0)
    for n in range(low + whole * by, high):
        body(n)


def take(values, index):
    return jnp.take_along_axis(values, index, axis=1, mode="promise_in_bounds")


def kernel(
    n_rows, n_cols, taps, scale,
    fl_hbm, fr_hbm, hid_hbm, g_hbm, wg_hbm, wc_hbm, disp_in, mw,
    nh, gl, gr,
    fl, fr, prev, left_in, disp_next, far_out, far_in, part_out, part_in, tap_out, tap_in,
    near1, tap_near, cols, disp, mwp,
    hb, gb, mb, in3, ci3, cg3, upd, rst, mpre, cbm,
    wg, wc, wcp, wct, wgp, edge_lo, edge_hi,
    local, send, recv,
):
    rid = lax.axis_index("rows")
    cid = lax.axis_index("cols")
    radius = taps // 2

    has = {
        ("rows", -1): rid > 0,
        ("rows", 1): rid < n_rows - 1,
        ("cols", -1): cid > 0,
        ("cols", 1): cid < n_cols - 1,
    }

    def target(axis, step):
        return (rid + step, cid) if axis == "rows" else (rid, cid + step)

    def message(n, src, dst, axis, step):
        return pltpu.make_async_remote_copy(
            src_ref=src, dst_ref=dst, send_sem=send.at[n], recv_sem=recv.at[n],
            device_id=target(axis, step), device_id_type=MESH,
        )

    def start(spec):
        @pl.when(has[spec[3], spec[4]])
        def _():
            message(*spec).start()

    def finish_send(spec):
        @pl.when(has[spec[3], spec[4]])
        def _():
            message(*spec).wait_send()

    def finish_recv(spec):
        @pl.when(has[spec[3], -spec[4]])
        def _():
            message(*spec).wait_recv()

    own = pl.ds(HALO, ROWS)
    main = pl.ds(0, COLS)
    copies = [
        pltpu.make_async_copy(src, dst, local.at[n])
        for n, (src, dst) in enumerate(
            [
                (fl_hbm, fl),
                (fr_hbm, fr),
                (hid_hbm, hb.at[own, main]),
                (g_hbm, gb.at[own, main]),
                (wg_hbm, wg),
                (wc_hbm, wc),
            ]
        )
    ]
    for copy in copies:
        copy.start()

    barrier = pltpu.get_barrier_semaphore()
    for (axis, step), there in has.items():
        @pl.when(there)
        def _(axis=axis, step=step):
            pl.semaphore_signal(barrier, inc=1, device_id=target(axis, step), device_id_type=MESH)
    peers = sum(there.astype(jnp.int32) for there in has.values())
    pl.semaphore_wait(barrier, peers)

    last = pl.ds(COLS - 16, 16)
    first = pl.ds(0, 16)
    col_msgs = [
        (0, hid_hbm.at[:, last], edge_lo.at[0], "cols", 1),
        (1, hid_hbm.at[:, first], edge_hi.at[0], "cols", -1),
        (2, g_hbm.at[:, last], edge_lo.at[1], "cols", 1),
        (3, g_hbm.at[:, first], edge_hi.at[1], "cols", -1),
    ]
    bands = pl.ds(0, BAND)
    tail_band = pl.ds(COLS - BAND, BAND)
    base = 17
    right_msgs, left_msgs, tap_msgs, slope_msgs, far_msgs, part_msgs = [], [], [], [], [], []
    for at, size in FWD_CHUNKS:
        rows = pl.ds(at, size)
        right_msgs.append((base, fr_hbm.at[rows, tail_band], prev.at[rows], "cols", 1))
        far_msgs.append((base + 1, far_out.at[rows], far_in.at[rows], "cols", -1))
        base += 2
    for at, size in BWD_CHUNKS:
        rows, whole = pl.ds(at, size), pl.ds(FWD + at, size)
        left_msgs.append((base, fl_hbm.at[whole, bands], left_in.at[rows], "cols", -1))
        tap_msgs.append((base + 1, tap_out.at[0, rows], tap_in.at[0, rows], "cols", 1))
        slope_msgs.append((base + 2, tap_out.at[1, rows], tap_in.at[1, rows], "cols", -1))
        part_msgs.append((base + 3, part_out.at[rows], part_in.at[rows], "cols", 1))
        base += 4
    disp_msg = (16, disp.at[pl.ds(FWD, BWD)], disp_next, "cols", -1)
    for r in range(ROWS):
        disp[r] = disp_in[r : r + 1, :]
    for spec in col_msgs + [disp_msg] + left_msgs + right_msgs:
        start(spec)
    mwp[...] = jnp.zeros_like(mwp)
    mwp[0:taps, :] = mw[...]

    def row_msgs(n, buf):
        return [
            (n, buf.at[pl.ds(HALO, HALO)], buf.at[pl.ds(HALO + ROWS, HALO)], "rows", -1),
            (n + 1, buf.at[pl.ds(ROWS, HALO)], buf.at[pl.ds(0, HALO)], "rows", 1),
        ]

    hid_rows, g_rows = row_msgs(8, hb), row_msgs(10, gb)
    motion_cols = [
        (12, mb.at[own, last], edge_lo.at[2], "cols", 1),
        (13, mb.at[own, first], edge_hi.at[2], "cols", -1),
    ]
    motion_rows = row_msgs(14, mb)
    @pl.when(jnp.logical_not(has["cols", -1]))
    def _():
        edge_lo[...] = jnp.zeros_like(edge_lo)
        prev[...] = jnp.zeros_like(prev)
        tap_in[0] = jnp.zeros(tap_in.shape[1:], BF)
        part_in[...] = jnp.zeros_like(part_in)

    @pl.when(jnp.logical_not(has["cols", 1]))
    def _():
        edge_hi[...] = jnp.zeros_like(edge_hi)
        far_in[...] = jnp.zeros_like(far_in)
        left_in[...] = jnp.zeros_like(left_in)
        disp_next[...] = jnp.zeros_like(disp_next)
        tap_in[1] = jnp.zeros(tap_in.shape[1:], BF)

    @pl.when(jnp.logical_not(has["rows", -1]))
    def _():
        for buf in (hb, gb, mb):
            buf[0:HALO] = jnp.zeros((HALO, WIDE, CH), BF)

    @pl.when(jnp.logical_not(has["rows", 1]))
    def _():
        for buf in (hb, gb, mb):
            buf[HALO + ROWS : EXT] = jnp.zeros((HALO, WIDE, CH), BF)

    side = lax.broadcasted_iota(jnp.int32, (16, CH), 0) < 8

    def join_edges(which, buf):
        def one(r):
            hi = edge_hi[which, r].astype(F32)
            lo = edge_lo[which, r].astype(F32)
            buf[HALO + r, COLS:WIDE, :] = jnp.where(side, hi, lo).astype(BF)

        loop(0, ROWS, one, 8)

    sub = lax.broadcasted_iota(jnp.int32, (BAND, BAND), 0)
    lane = lax.broadcasted_iota(jnp.int32, (BAND, BAND), 1)
    ones = jnp.ones((BAND, BAND), BF)

    turn = (lax.broadcasted_iota(jnp.int32, (TAP_PAD, BAND), 0) == lax.broadcasted_iota(jnp.int32, (TAP_PAD, BAND), 1)).astype(BF)
    back = (sub == lane).astype(BF)[0:TAP_PAD]

    def spread_line(line):
        diag = jnp.where(sub == lane, line.astype(F32), 0.0).astype(BF)
        return mm(diag, ones).astype(jnp.int32)

    def column_of(line):
        return sub + radius - spread_line(line) - lane

    def usable_of(col):
        level = sub - col
        return (level >= 0) & (level < BAND) & (lane < taps)

    def pick(values, col):
        return take(values, col & (BAND - 1))

    def g_of(picked, col, shift):
        return jnp.where(((col + shift) & -TAP_PAD) == 0, picked, 0.0).astype(BF)

    def finish_motion(r, b, pre):
        mpre[r, b * BAND : (b + 1) * BAND, :] = pre
        mb[HALO + r, b * BAND : (b + 1) * BAND, :] = (pre * sig(pre)).astype(BF)

    def near_row(n):
        for s in range(4):
            near_one(4 * n + s)

    def near_one(r):
        c0 = column_of(disp[r, :, 0:BAND])
        c1 = column_of(disp[r, :, BAND:COLS])
        cols[0, r] = c0
        cols[1, r] = c1
        near = pick(mm_nt(fl[r, 0:BAND, :], fr[r, 0:BAND, :]), c0)
        tap_near[r] = jnp.where((c0 >= 0) & usable_of(c0), near, 0.0) * scale
        both = mm_nt(fl[r, BAND:COLS, :], fr[r])
        tap = jnp.where(c1 >= 0, pick(both[:, BAND:], c1), pick(both[:, :BAND], c1))
        tap = jnp.where(usable_of(c1), tap, 0.0) * scale
        finish_motion(r, 1, mm(tap.astype(BF), mwp[...]))

    for copy in copies[:2]:
        copy.wait()
    loop(0, ROWS // 4, near_row, 1)
    start(motion_cols[0])
    for copy in copies[2:4]:
        copy.wait()
    for spec in col_msgs:
        finish_recv(spec)
    join_edges(0, hb)
    join_edges(1, gb)
    for spec in hid_rows + g_rows:
        start(spec)

    for copy in copies[4:]:
        copy.wait()
    wcp[...] = jnp.zeros_like(wcp)
    wgp[...] = jnp.zeros_like(wgp)
    for a in range(3):
        for b in range(3):
            t = a * 3 + b
            blk = wc[t * 256 : (t + 1) * 256, :]
            wcp[a * 768 + b * 256 : a * 768 + (b + 1) * 256, 0:CH] = blk
            wcp[(a + 1) * 768 + b * 256 : (a + 1) * 768 + (b + 1) * 256, CH : 2 * CH] = blk
            wct[t * CH : (t + 1) * CH, :] = blk.astype(F32).T.astype(BF)
            turned = wg[t * 256 + CH : (t + 1) * 256, :].astype(F32).T.astype(BF)
            q = 2 - a
            wgp[q * 768 + b * 256 : q * 768 + (b + 1) * 256, 0:CH] = turned
            wgp[(q + 1) * 768 + b * 256 : (q + 1) * 768 + (b + 1) * 256, CH : 2 * CH] = turned


    for spec in hid_rows + g_rows:
        finish_recv(spec)

    def fill_hidden(r):
        put3(((in3, r),), 0, 256, hb[r].astype(F32), True)

    loop(0, EXT, fill_hidden, 4)

    def far_row(r):
        c0 = cols[0, r]
        far = pick(mm_nt(fl[r, 0:BAND, :], prev[r]), c0) * scale
        tap = jnp.where((c0 < 0) & usable_of(c0), far, tap_near[r])
        finish_motion(r, 0, mm(tap.astype(BF), mwp[...]))

    def next_row(i):
        c = column_of(disp_next[i, :, 0:BAND])
        far = pick(mm_nt(left_in[i], fr[FWD + i, BAND:COLS, :]), c) * scale
        tap = jnp.where((c < 0) & usable_of(c), far, 0.0).astype(BF)
        tap_out[0, i] = mm_nt(turn, tap).astype(BF)

    def taken_row(i):
        pre = mm(tap_near[FWD + i].astype(BF), mwp[...])
        finish_motion(FWD + i, 0, pre + mm_tn(tap_in[0, i], mwp[0:TAP_PAD, :]))

    def over(chunk, body):
        loop(chunk[0], chunk[0] + chunk[1], body, chunk[1])

    finish_recv(disp_msg)
    for n, chunk in enumerate(BWD_CHUNKS):
        finish_recv(right_msgs[n])
        over(FWD_CHUNKS[n], far_row)
        finish_recv(left_msgs[n])
        over(chunk, next_row)
        start(tap_msgs[n])
    for n in range(len(BWD_CHUNKS), len(FWD_CHUNKS)):
        finish_recv(right_msgs[n])
        over(FWD_CHUNKS[n], far_row)
    for n, chunk in enumerate(BWD_CHUNKS):
        finish_recv(tap_msgs[n])
        over(chunk, taken_row)

    start(motion_cols[1])
    for spec in motion_cols:
        finish_recv(spec)
    join_edges(2, mb)
    for spec in motion_rows:
        start(spec)

    def fill_motion(r):
        m = mb[r].astype(F32)
        put3(((in3, r), (ci3, r - 1)), 1, 256, m, True)

    def rows_of(ref, r, count):
        return ref[pl.ds(r, count)].reshape(count * WIDE, ref.shape[2])

    def gate_pair(r):
        acc = mm(jnp.concatenate([rows_of(in3, r + a, 2) for a in (-1, 0, 1)], axis=1), wg[...])
        for s in range(2):
            part = acc[s * WIDE : (s + 1) * WIDE]
            reset = sig(part[:, CH:])
            upd[r + s - 1] = sig(part[:, :CH])
            rst[r + s - 1] = reset
            put3(((ci3, r + s - 1),), 0, 256, reset * hb[r + s].astype(F32), True)

    loop(HALO, HALO + ROWS, fill_motion, 4)
    loop(0, ROWS // 2 - 1, lambda n: gate_pair(HALO + 1 + 2 * n), 2)
    for spec in motion_rows:
        finish_recv(spec)
    mb_top = EXT - 1
    loop(1, HALO, fill_motion, HALO - 1)
    loop(HALO + ROWS, mb_top, fill_motion, HALO - 1)
    put3(((in3, 0),), 1, 256, mb[0].astype(F32), True)
    put3(((in3, mb_top),), 1, 256, mb[mb_top].astype(F32), True)
    loop(0, 2, lambda n: gate_pair(1 + 2 * n), 2)
    loop(0, 2, lambda n: gate_pair(HALO + ROWS - 1 + 2 * n), 2)

    def cand_quad(n, kept):
        r = 2 + 4 * n
        acc = None
        for q in range(4):
            lhs = jnp.concatenate([ci3[r - 2 + q], ci3[r + q]], axis=0)
            term = mm(lhs, wcp[q * 768 : (q + 1) * 768, :])
            acc = term if acc is None else acc + term
        for s in range(4):
            c = jnp.tanh(acc[(s // 2) * WIDE : (s // 2 + 1) * WIDE, (s % 2) * CH : (s % 2 + 1) * CH])
            u = upd[r + s - 1]
            h = hb[r + s].astype(F32)
            g = gb[r + s].astype(F32)
            if kept[s]:
                nh[r + s - HALO] = ((1.0 - u) * h + u * c)[:COLS].astype(BF)
            put3(((cg3, r + s - 2),), 0, CH, g * u * (1.0 - c * c), False)
            put3(((in3, r + s),), 0, 256, g * (c - h) * u * (1.0 - u), False)

    cand_quad(0, (False, False, True, True))
    loop(1, 4, lambda n: cand_quad(n, (True,) * 4), 1)
    cand_quad(4, (True, True, False, False))

    def back_pair(n):
        r = HALO - 1 + 2 * n
        acc = mm(jnp.concatenate([rows_of(cg3, r - a, 2) for a in (1, 2, 3)], axis=1), wct[...])
        for s in range(2):
            part = acc[s * WIDE : (s + 1) * WIDE]
            reset = rst[r + s - 1]
            grad = part[:, :CH] * hb[r + s].astype(F32) * reset * (1.0 - reset)
            put3(((in3, r + s),), 1, 256, grad, False)
            cbm[r + s - 3] = part[:, CH:]

    loop(0, ROWS // 2 + 1, back_pair, 3)

    def slopes(n, b, store):
        r = HALO + 4 * n
        cut = slice(b * BAND, (b + 1) * BAND)
        acc = None
        for q in range(4):
            lhs = jnp.concatenate([in3[r - 1 + q, cut], in3[r + 1 + q, cut]], axis=0)
            term = mm(lhs, wgp[q * 768 : (q + 1) * 768, :])
            acc = term if acc is None else acc + term
        for s in range(4):
            row = 4 * n + s
            half = acc[(s // 2) * BAND : (s // 2 + 1) * BAND, (s % 2) * CH : (s % 2 + 1) * CH]
            motion_grad = half + cbm[row + 1, cut]
            pre = mpre[row, cut]
            sg = sig(pre)
            pre_grad = (motion_grad * sg * (1.0 + pre * (1.0 - sg))).astype(BF)
            col = cols[b, row]
            tap = jnp.where(usable_of(col), mm_nt(pre_grad, mwp[...]), 0.0)
            store(row, col, tap)

    def keep_tap(row, col, tap):
        tap_near[row] = pick(tap, col)
        if row >= FWD:
            tap_out[1, row - FWD] = mm_nt(turn, tap.astype(BF)).astype(BF)

    def send_far(r):
        g_far = g_of(tap_near[r], cols[0, r], BAND)
        far_out[r] = (mm_tn(g_far, fl[r, 0:BAND, :]) * scale).astype(BF)

    def send_part(i):
        col = column_of(disp_next[i, :, 0:BAND])
        g_far = g_of(pick(mm_tn(tap_in[1, i], back), col), col, BAND)
        part_out[i] = (mm(g_far, fr[FWD + i, BAND:COLS, :]) * scale).astype(BF)
        near1[FWD + i] = mm_tn(g_far, left_in[i]) * scale

    def own_second(row, col, tap):
        picked = pick(tap, col)
        g_both = jnp.concatenate([g_of(picked, col, BAND), g_of(picked, col, 0)], axis=1)
        gl[row, BAND:COLS, :] = (mm(g_both, fr[row]) * scale).astype(BF)
        grads = mm_tn(g_both, fl[row, BAND:COLS, :]) * scale
        col0 = cols[0, row]
        g_first = g_of(tap_near[row], col0, 0)
        far = grads[:BAND].astype(BF).astype(F32)
        gr[row, 0:BAND, :] = (mm_tn(g_first, fl[row, 0:BAND, :]) * scale + far).astype(BF)
        near = grads[BAND:]
        first = mm(g_first, fr[row, 0:BAND, :])

        if row < FWD:
            g_back = g_of(tap_near[row], col0, BAND)
            gl[row, 0:BAND, :] = ((first + mm(g_back, prev[row])) * scale).astype(BF)
            near1[row] = near
        else:
            gr[row, BAND:COLS, :] = (near + near1[row].astype(BF).astype(F32)).astype(BF)
            near1[row] = first * scale

    quads = ROWS // 4
    split = FWD // 4
    for n in range(split, quads):
        slopes(n, 0, keep_tap)
    for spec in slope_msgs:
        start(spec)
    for n in range(split):
        slopes(n, 0, keep_tap)
    for n, chunk in enumerate(FWD_CHUNKS):
        over(chunk, send_far)
        start(far_msgs[n])
    for n, chunk in enumerate(BWD_CHUNKS):
        finish_recv(slope_msgs[n])
        over(chunk, send_part)
        start(part_msgs[n])
    for n in range(quads):
        slopes(n, 1, own_second)

    def add_far(r):
        gr[r, BAND:COLS, :] = (near1[r] + far_in[r].astype(F32)).astype(BF)

    def add_part(i):
        gl[FWD + i, 0:BAND, :] = (near1[FWD + i] + part_in[i].astype(F32)).astype(BF)

    for n, chunk in enumerate(FWD_CHUNKS):
        finish_recv(far_msgs[n])
        over(chunk, add_far)
    for n, chunk in enumerate(BWD_CHUNKS):
        finish_recv(part_msgs[n])
        over(chunk, add_part)
    sent = col_msgs + [disp_msg] + left_msgs + right_msgs + hid_rows + g_rows + motion_cols + motion_rows
    for spec in sent + tap_msgs + slope_msgs + far_msgs + part_msgs:
        finish_send(spec)


def hand_on(*refs):
    half = len(refs) // 2
    for src, dst in zip(refs[:half], refs[half:]):
        dst[...] = src[...]


def whole_copy(*arrays):
    specs = [pl.BlockSpec((4,) + a.shape[1:], lambda i: (i, 0, 0)) for a in arrays]
    return pl.pallas_call(
        hand_on,
        grid=(ROWS // 4,),
        out_shape=tuple(jax.ShapeDtypeStruct(a.shape, a.dtype) for a in arrays),
        in_specs=specs,
        out_specs=tuple(specs),
    )(*arrays)


def per_device(n_rows, n_cols, feat_left, feat_right, hidden, disparity, motion_weight, gate_weight, cand_weight, grad_hidden):
    taps = motion_weight.shape[0]
    feat = feat_left.shape[2]
    wg = gate_weight.reshape(9 * 256, 256)
    wc = cand_weight.reshape(9 * 256, CH)
    hbm = pl.BlockSpec(memory_space=pl.ANY)
    vmem = pl.BlockSpec(memory_space=pltpu.VMEM)
    v = pltpu.VMEM
    outs = pl.pallas_call(
        functools.partial(kernel, n_rows, n_cols, taps, 1.0 / math.sqrt(feat)),
        out_shape=(
            jax.ShapeDtypeStruct(hidden.shape, BF),
            jax.ShapeDtypeStruct(feat_left.shape, BF),
            jax.ShapeDtypeStruct(feat_right.shape, BF),
        ),
        in_specs=[hbm] * 6 + [vmem] * 2,
        out_specs=(vmem,) * 3,
        scratch_shapes=[
            v((ROWS, COLS, feat), BF),
            v((ROWS, COLS, feat), BF),
            v((FWD, BAND, feat), BF),
            v((BWD, BAND, feat), BF),
            v((BWD, 1, COLS), jnp.int32),
            v((FWD, BAND, feat), BF),
            v((FWD, BAND, feat), BF),
            v((BWD, BAND, feat), BF),
            v((BWD, BAND, feat), BF),
            v((2, BWD, TAP_PAD, BAND), BF),
            v((2, BWD, TAP_PAD, BAND), BF),
            v((ROWS, BAND, feat), F32),
            v((ROWS, BAND, BAND), F32),
            v((2, ROWS, BAND, BAND), jnp.int32),
            v((ROWS, 1, COLS), jnp.int32),
            v((BAND, CH), BF),
            v((EXT, WIDE, CH), BF),
            v((EXT, WIDE, CH), BF),
            v((EXT, WIDE, CH), BF),
            v((EXT, WIDE, 6 * CH), BF),
            v((EXT - 2, WIDE, 6 * CH), BF),
            v((EXT - 4, WIDE, 3 * CH), BF),
            v((EXT - 2, WIDE, CH), F32),
            v((EXT - 2, WIDE, CH), F32),
            v((ROWS, COLS, CH), F32),
            v((ROWS + 2, WIDE, CH), F32),
            v((9 * 256, 256), BF),
            v((9 * 256, CH), BF),
            v((12 * 256, 256), BF),
            v((9 * CH, 256), BF),
            v((12 * 256, 256), BF),
            v((3, ROWS, 16, CH), BF),
            v((3, ROWS, 16, CH), BF),
            pltpu.SemaphoreType.DMA((6,)),
            pltpu.SemaphoreType.DMA((N_MSG,)),
            pltpu.SemaphoreType.DMA((N_MSG,)),
        ],
        compiler_params=pltpu.CompilerParams(
            collective_id=0, has_side_effects=True, vmem_limit_bytes=63 * 1024 * 1024
        ),
        cost_estimate=pl.CostEstimate(flops=17 * 10**9, bytes_accessed=14 * 10**6, transcendentals=0),
    )(feat_left, feat_right, hidden, grad_hidden, wg, wc, disparity, motion_weight)
    return whole_copy(*outs)


def solution(mesh):
    blocks = P("rows", "cols", None)
    return jax.shard_map(
        functools.partial(per_device, mesh.shape["rows"], mesh.shape["cols"]),
        mesh=mesh,
        in_specs=(blocks, blocks, blocks, P("rows", "cols"), P(), P(), P(), blocks),
        out_specs=(blocks, blocks, blocks),
        check_vma=False,
    )
```
